256 devices in a mesh: head: 4 (over y_hi, core), ctx: 64 (over x, y_lo, z).
Axes of the slice: x: 4, y: 4 (y_hi: 2, y_lo: 2; y = y_hi * 2 + y_lo), z: 8, core: 2. Of those that a mesh axis runs over, the one named last changes fastest.
Arguments:
- q_new: bfloat16 [512, 8192], P(('head', 'ctx')), may hold values from -20 to 20
- kv_new: bfloat16 [512, 2048], P(('head', 'ctx')), may hold values from -4 to 4
- k_cache: bfloat16 [8, 131072, 128], P('head', 'ctx'), may hold values from -4 to 4
- v_cache: bfloat16 [8, 131072, 128], P('head', 'ctx'), may hold values from -4 to 4
- span_len: int32 [64], P('ctx'), may hold values from 1 to 2048, 81920 in all
- order: int32 [512], replicated, may hold values from 0 to 511, each once
Outputs:
- attended: bfloat16 [512, 8192], P(('head', 'ctx'))
The draws below stay inside these ranges and needn't reach their ends.
Inputs may be any that keep to these rules, and one draw needn't show every extreme that they name: `span_len`: in every span at least one slot is valid, and some span is full. `order`: each position appears once.
All inputs are finite; a program needn't handle non-finite values. No bound on the sum of `span_len` on one device may be relied on, other than what follows from the above.
Results may differ from the reference program's by a relative error of at most 0.002.
Values may be sent and summed in bfloat16 or wider, within the bound.
A program may use at most 64 MiB of HBM per device.

```python
import math
import jax
import jax.numpy as jnp
import numpy as np
from jax import lax

HQ = 64
KVH = 8
HD = 128
NEW = 512
CTX_DEV = 2048
SPANS = 64
CTX = 131072
SHARE = 128
TL = 2
N_HEAD = 4


def draw_q_new(key, part):
    key = jax.random.fold_in(key, 11)
    first = jax.random.fold_in(key, 0)
    values = jnp.clip(jax.random.normal(first, (NEW, HQ * HD), jnp.float32) * 2.5, -15.0, 15.0)
    return values.astype(jnp.bfloat16)


def draw_k_cache(key, part):
    key = jax.random.fold_in(key, 23)
    values = jnp.clip(jax.random.normal(key, (KVH, CTX, HD), jnp.float32), -4.0, 4.0)
    return values.astype(jnp.bfloat16)


def block_scale(rng, dims, cuts, least, largest):
    def one(position, blocks):
        draws = jax.random.uniform(jax.random.fold_in(jax.random.fold_in(rng, 6), position), (blocks,), jnp.float32, least / len(cuts), largest / len(cuts))
        return jnp.repeat(jnp.exp(draws), dims[position] // blocks).reshape((-1,) + (1,) * (len(dims) - position - 1))

    loudness = one(*cuts[0])
    for cut in cuts[1:]:
        loudness = loudness * one(*cut)
    return loudness


def profile(number_of, total, limit, skew):
    portions = [(1 << 20) // math.isqrt(grade ** skew) + 1 for grade in range(2, number_of + 1)]
    rest, counts = total - limit - (number_of - 1), [1] * (number_of - 1)
    while rest > 0:
        free = [i for i in range(number_of - 1) if counts[i] < limit]
        whole, remaining = sum([portions[i] for i in free]), rest
        for i in free:
            more = min(limit - counts[i], max(1, remaining * portions[i] // whole), rest)
            counts[i] = counts[i] + more
            rest = rest - more
    return np.array([limit] + counts)


def uneven(own_key, amount, total, most, skew):
    if amount == 2:
        one = jax.random.randint(own_key, (), max(1, total - most), min(most, total - 1) + 1)
        return jnp.stack([one, total - one])
    tallies = jnp.asarray(profile(amount, total, most, skew), jnp.int32)
    twos = (amount - 1) // 2
    giver, taker = tallies[1:1 + 2 * twos:2], tallies[2:2 + 2 * twos:2]
    slack = jnp.minimum(giver - 1, most - taker)
    moved = jax.random.randint(jax.random.fold_in(own_key, 1), (twos,), 0, 1 << 20) % (slack + 1)
    tallies = tallies.at[1:1 + 2 * twos:2].set(giver - moved).at[2:2 + 2 * twos:2].set(taker + moved)
    return tallies[jax.random.permutation(jax.random.fold_in(own_key, 2), amount)]


def scatter_about(stream_key, extent, deviation, limit, cuts=(), held_as=jnp.bfloat16):
    array = jax.random.normal(stream_key, extent, jnp.float32) * deviation
    if len(cuts) > 0:
        array = block_scale(stream_key, extent, cuts, -0.22, 0.18) * array
    return jnp.clip(array, min=-limit, max=limit).astype(held_as)


def setup_inputs(seed: int = 0) -> dict:
    key_list = jax.random.split(jax.random.key(seed), 7)
    q_new = draw_q_new(jax.random.fold_in(key_list[6], 71), 0)
    kv_new = scatter_about(key_list[1], (NEW, KVH * 2 * HD), 1.0, 4.0, ((0, 256),))
    k_cache = draw_k_cache(jax.random.fold_in(key_list[6], 71), 0)
    v_cache = scatter_about(key_list[3], (KVH, CTX, HD), 1.0, 4.0, ((0, 4), (1, 64)))
    span_len = uneven(key_list[4], SPANS, SPANS * CTX_DEV * 5 // 8, CTX_DEV, 2).astype(jnp.int32)
    order = jax.random.permutation(key_list[5], NEW).astype(jnp.int32)
    return {"q_new": q_new, "kv_new": kv_new, "k_cache": k_cache, "v_cache": v_cache, "span_len": span_len, "order": order}


masked = -1.0e30


def reference(q_new, kv_new, k_cache, v_cache, span_len, order):
    group = HQ // KVH
    scale = HD ** -0.5
    queries = q_new.astype(jnp.float32).reshape(NEW, KVH, group, HD)
    fresh = kv_new.reshape(NEW, KVH, 2, HD)
    keys_fresh = fresh[:, :, 0, :]
    values_fresh = fresh[:, :, 1, :]

    def one_span(carry, span):
        best, acc_out, acc_total = carry
        start = (span * CTX_DEV).astype(jnp.int32)
        keys_span = lax.dynamic_slice_in_dim(k_cache, start, CTX_DEV, 1).astype(jnp.float32)
        values_span = lax.dynamic_slice_in_dim(v_cache, start, CTX_DEV, 1).astype(jnp.float32)
        token_ids = (jnp.arange(N_HEAD, dtype=jnp.int32)[:, None] * SHARE + span * TL
                     + jnp.arange(TL, dtype=jnp.int32)[None, :]).reshape(-1).astype(jnp.int32)
        keys_new = jnp.take(keys_fresh, token_ids, axis=0).astype(jnp.float32)
        values_new = jnp.take(values_fresh, token_ids, axis=0).astype(jnp.float32)
        key_order = jnp.take(order, token_ids, axis=0)
        s_cached = jnp.einsum("qkgd,ksd->qkgs", queries, keys_span) * scale
        valid = jnp.arange(CTX_DEV, dtype=jnp.int32) < span_len[span]
        s_cached = jnp.where(valid[None, None, None, :], s_cached, masked)
        s_fresh = jnp.einsum("qkgd,tkd->qkgt", queries, keys_new) * scale
        seen = key_order[None, :] <= order[:, None]
        s_fresh = jnp.where(seen[:, None, None, :], s_fresh, masked)
        peak = jnp.maximum(jnp.max(s_cached, -1), jnp.max(s_fresh, -1))
        p_cached = jnp.exp(s_cached - peak[..., None])
        p_fresh = jnp.exp(s_fresh - peak[..., None])
        total = jnp.sum(p_cached, -1) + jnp.sum(p_fresh, -1)
        pc_round = lax.optimization_barrier(p_cached.astype(jnp.bfloat16)).astype(jnp.float32)
        pf_round = lax.optimization_barrier(p_fresh.astype(jnp.bfloat16)).astype(jnp.float32)
        part = jnp.einsum("qkgs,ksd->qkgd", pc_round, values_span) + jnp.einsum("qkgt,tkd->qkgd", pf_round, values_new)
        new_best = jnp.maximum(best, peak)
        keep = jnp.exp(best - new_best)
        take = jnp.exp(peak - new_best)
        acc_out = acc_out * keep[..., None] + part * take[..., None]
        acc_total = acc_total * keep + total * take
        return (new_best, acc_out, acc_total), None

    start_best = jnp.full((NEW, KVH, group), masked, jnp.float32)
    start_out = jnp.zeros((NEW, KVH, group, HD), jnp.float32)
    start_total = jnp.zeros((NEW, KVH, group), jnp.float32)
    (best, acc_out, acc_total), _ = lax.scan(one_span, (start_best, start_out, start_total), jnp.arange(SPANS, dtype=jnp.int32))
    result = acc_out / acc_total[..., None]
    return result.reshape(NEW, HQ * HD).astype(jnp.bfloat16)
```

```python
import functools

import jax
import jax.numpy as jnp
from jax import lax
from jax.experimental import pallas as pl
from jax.experimental.pallas import tpu as pltpu
from jax.sharding import PartitionSpec as P

MESH = pl.DeviceIdType.MESH
masked = -1e30
NH = 4
NY = 2
COL = NH * NY
CHUNK = 256


def kernel(
    nx, nz, scale2,
    msg, ordq, lens, k_hbm, v_hbm,
    out,
    col, qall, kb, vb, vt, kf, vf, fresh_f, bias, plen, s_a, s_b, acc, part, xin, zpart, zin, fin, fout,
    col_s, col_r, len_s, len_r, kv_s, kv_r, own_sem, qz_s, qz_r, qx_s, qx_r,
    px_s, px_r, pz_s, pz_r, f_s, f_r,
):
    h = lax.axis_index("head")
    c = lax.axis_index("ctx")
    z = lax.rem(c, nz)
    y = lax.rem(lax.div(c, nz), NY)
    x = lax.div(c, nz * NY)
    u = y * NH + h
    slots = k_hbm.shape[1]
    rows = 128 * nx
    chunks = slots // CHUNK

    def at(h_, x_, y_, z_):
        return (h_, (x_ * NY + y_) * nz + z_)

    def col_peer(off):
        w = lax.rem(u + off, COL)
        return w, lax.rem(w, NH), lax.div(w, NH)

    def remote(src, dst, ss, rs, dev):
        return pltpu.make_async_remote_copy(
            src_ref=src, dst_ref=dst, send_sem=ss, recv_sem=rs, device_id=dev, device_id_type=MESH
        )

    def far(t):
        half = lax.div(t, 2)
        return jnp.where(lax.rem(t, 2) == 0, nz // 2 + half, nz // 2 - 1 - half)

    def plane(t):
        return lax.rem(z + far(t), nz)

    own = [
        pltpu.make_async_copy(k_hbm.at[y], kb.at[0], own_sem.at[0]),
        pltpu.make_async_copy(v_hbm.at[y], vb.at[0], own_sem.at[1]),
    ]
    for copy in own:
        copy.start()

    barrier = pltpu.get_barrier_semaphore()
    for off in range(1, COL):
        _, h_, y_ = col_peer(off)
        pl.semaphore_signal(barrier, inc=1, device_id=at(h_, x, y_, z), device_id_type=MESH)
    for off in range(1, nz):
        pl.semaphore_signal(
            barrier, inc=1, device_id=at(h, x, y, lax.rem(z + off, nz)), device_id_type=MESH
        )
    for off in range(1, nx):
        pl.semaphore_signal(
            barrier, inc=1, device_id=at(h, lax.rem(x + off, nx), y, z), device_id_type=MESH
        )
    pl.semaphore_wait(barrier, COL + nz + nx - 3)

    def col_copy(off):
        w, h_, y_ = col_peer(off)
        return remote(
            msg.at[NY * h_ + y_], col.at[u], col_s.at[w], col_r.at[u], at(h_, x, y_, z)
        )

    def col_arrival(off):
        w, h_, y_ = col_peer(off)
        return remote(msg.at[0], col.at[w], col_s.at[w], col_r.at[w], at(h_, x, y_, z))

    for off in range(1, COL):
        col_copy(off).start()
    partner = at(h, x, 1 - y, z)
    len_copy = remote(lens, plen, len_s, len_r, partner)
    len_copy.start()
    col[u] = msg[NY * h + y]
    for off in range(1, COL):
        col_arrival(off).wait_recv()

    base = pl.multiple_of(x * 128, 128)
    for w in range(COL):
        qall[z, pl.ds(pl.multiple_of(x * 128 + w * 16, 16), 16), :] = col[w, 0:16, :]

    def qz_copy(t):
        to = lax.rem(z + nz - far(t), nz)
        ref = qall.at[z, pl.ds(base, 128), :]
        return remote(ref, ref, qz_s.at[t], qz_r.at[t], at(h, x, y, to))

    def qz_arrival(t):
        ref = qall.at[plane(t), pl.ds(base, 128), :]
        return remote(ref, ref, qz_s.at[t], qz_r.at[t], at(h, x, y, plane(t)))

    def qx_copy(t, off):
        ref = qall.at[plane(t), pl.ds(base, 128), :]
        return remote(
            ref, ref, qx_s.at[t, off], qx_r.at[t, off], at(h, lax.rem(x + off, nx), y, z)
        )

    def qx_arrival(t, off):
        who = lax.rem(x + nx - off, nx)
        ref = qall.at[plane(t), pl.ds(pl.multiple_of(who * 128, 128), 128), :]
        return remote(ref, ref, qx_s.at[t, off], qx_r.at[t, off], at(h, who, y, z))

    for t in range(nz - 1):
        qz_copy(t).start()
    kv = [
        remote(k_hbm.at[1 - y], kb.at[1], kv_s.at[0], kv_r.at[0], partner),
        remote(v_hbm.at[1 - y], vb.at[1], kv_s.at[1], kv_r.at[1], partner),
    ]
    for copy in kv:
        copy.start()

    for span in range(2):
        side = y if span == 0 else 1 - y
        fresh_f[...] = jnp.zeros_like(fresh_f)
        for w in range(NH):
            block = col[side * NH + w, 16:32, :].astype(jnp.float32)
            fresh_f[0, 2 * w : 2 * w + 2, :] = block[0:2, :]
            fresh_f[1, 2 * w : 2 * w + 2, :] = block[2:4, :]
        kf[span] = fresh_f[0].astype(jnp.bfloat16)
        vf[span] = fresh_f[1].astype(jnp.bfloat16)

    def set_bias(span, length):
        for j in range(chunks):
            slot = lax.broadcasted_iota(jnp.int32, (CHUNK, 128), 0).astype(jnp.float32) + j * CHUNK
            bias[span, j * CHUNK : (j + 1) * CHUNK, :] = jnp.where(slot < length, 0.0, masked)

    def turn(span):
        for j in range(slots // 128):
            vt[span, :, j * 128 : (j + 1) * 128] = vb[span, j * 128 : (j + 1) * 128, :].T

    set_bias(0, lens[0:1, :])
    for copy in own:
        copy.wait()
    turn(0)

    tile_row = lax.broadcasted_iota(jnp.int32, (8, 128), 0)
    for d in range(nz):
        for w in range(nx):
            part[d, w, 0:128, :] = jnp.zeros((128, 128), jnp.float32)
            part[d, w, 128:136, :] = jnp.where(tile_row == 0, masked, 0.0)

    mine = ordq[z, :, pl.ds(base, 128)]
    lane = lax.broadcasted_iota(jnp.int32, (8, 128), 1)

    def key_order(side):
        hit = lax.div(lane, 8) == tile_row + 8 * side
        return jnp.max(jnp.where(hit, mine, -1.0), axis=1, keepdims=True)

    fresh_order = (key_order(y), key_order(1 - y))

    for t in range(nz - 1):
        qz_arrival(t).wait_recv()
        for off in range(1, nx):
            qx_copy(t, off).start()
    for off in range(1, nx):
        qx_copy(nz - 1, off).start()

    def scores(span, d, s_ref, j, m):
        keys = kb[span, j * CHUNK : (j + 1) * CHUNK, :]
        s = lax.dot_general(
            keys, qall[d], (((1,), (1,)), ((), ())), preferred_element_type=jnp.float32
        )
        s = s + jnp.concatenate([bias[span, j * CHUNK : (j + 1) * CHUNK, :]] * nx, axis=1)
        s_ref[j * CHUNK : (j + 1) * CHUNK, :] = s
        top = jnp.max(s.reshape(CHUNK // 8, 8, rows), axis=0)
        return top if m is None else jnp.maximum(m, top)

    def fresh_scores(span, d, s_ref, m):
        s = lax.dot_general(
            kf[span], qall[d], (((1,), (1,)), ((), ())), preferred_element_type=jnp.float32
        )
        key = jnp.where(span == 0, fresh_order[0], fresh_order[1])
        s = jnp.where(key <= ordq[d], s[0:8, :], masked)
        s_ref[slots : slots + 8, :] = s
        return jnp.maximum(m, s)

    def weights(span, s_ref, j, peak, total):
        p = jnp.exp2(s_ref[j * CHUNK : (j + 1) * CHUNK, :] * scale2 - peak)
        total = total + jnp.sum(p.reshape(CHUNK // 8, 8, rows), axis=0)
        values = vt[span, :, j * CHUNK : (j + 1) * CHUNK]
        more = jnp.dot(values, p.astype(jnp.bfloat16), preferred_element_type=jnp.float32)
        if j == 0:
            acc[...] = more
        else:
            acc[...] += more
        return total

    def fresh_weights(span, s_ref, peak, total):
        p = jnp.exp2(s_ref[slots : slots + 8, :] * scale2 - peak)
        both = jnp.concatenate([p, jnp.zeros_like(p)], axis=0).astype(jnp.bfloat16)
        acc[...] += lax.dot_general(
            vf[span], both, (((0,), (0,)), ((), ())), preferred_element_type=jnp.float32
        )
        return total + p

    def add_part(d, peak, total):
        total = jnp.sum(total, axis=0, keepdims=True)
        for w in range(nx):
            cut = slice(w * 128, (w + 1) * 128)
            old = part[d, w, 128:136, :]
            new_peak = jnp.maximum(old[0:1, :], peak[:, cut])
            keep = jnp.exp2(old[0:1, :] - new_peak)
            take = jnp.exp2(peak[:, cut] - new_peak)
            part[d, w, 0:128, :] = part[d, w, 0:128, :] * keep + acc[:, cut] * take
            new_total = old[1:2, :] * keep + total[:, cut] * take
            part[d, w, 128:136, :] = jnp.where(tile_row == 0, new_peak, new_total)

    def step(t, s_now, s_next, m, ahead):
        span = lax.div(t, nz)
        d = plane(lax.rem(t, nz))
        span_n = lax.div(t + 1, nz)
        d_n = plane(lax.rem(t + 1, nz))
        peak = jnp.max(m, axis=0, keepdims=True) * scale2
        total = jnp.zeros((8, rows), jnp.float32)
        nxt = None
        for j in range(chunks):
            if ahead:
                nxt = scores(span_n, d_n, s_next, j, nxt)
            total = weights(span, s_now, j, peak, total)
        if ahead:
            nxt = fresh_scores(span_n, d_n, s_next, nxt)
        total = fresh_weights(span, s_now, peak, total)
        add_part(d, peak, total)
        return nxt

    def px_copy(t, off):
        who = lax.rem(x + off, nx)
        d = plane(t)
        return remote(part.at[d, who], xin.at[d, x], px_s.at[t, off], px_r.at[t, off], at(h, who, y, z))

    def px_arrival(t, off):
        who = lax.rem(x + nx - off, nx)
        d = plane(t)
        return remote(part.at[d, who], xin.at[d, who], px_s.at[t, off], px_r.at[t, off], at(h, who, y, z))

    def pz_copy(t):
        d = plane(t)
        return remote(zpart.at[d], zin.at[t], pz_s.at[t], pz_r.at[t], at(h, x, y, d))

    def pz_arrival(t):
        who = lax.rem(z + nz - far(t), nz)
        return remote(zpart.at[who], zin.at[t], pz_s.at[t], pz_r.at[t], at(h, x, y, who))

    def merged(tiles, blocks):
        peak = functools.reduce(jnp.maximum, [tile[0:1, :] for tile in tiles])
        factors = [jnp.exp2(tile[0:1, :] - peak) for tile in tiles]
        total = sum(tile[1:2, :] * f for tile, f in zip(tiles, factors))
        value = sum(block * f for block, f in zip(blocks, factors))
        return peak, total, value

    def merge_x(t):
        d = plane(t)
        for off in range(1, nx):
            px_arrival(t, off).wait_recv()
        tiles, blocks = [part[d, x, 128:136, :]], [part[d, x, 0:128, :]]
        for off in range(1, nx):
            who = lax.rem(x + off, nx)
            tiles.append(xin[d, who, 128:136, :])
            blocks.append(xin[d, who, 0:128, :])
        peak, total, value = merged(tiles, blocks)
        zpart[d, 0:128, :] = value
        zpart[d, 128:136, :] = jnp.where(tile_row == 0, peak, total)

    def need_q(t):
        for off in range(1, nx):
            qx_arrival(t, off).wait_recv()

    def before(t):
        @pl.when(t + 1 < nz)
        def _():
            need_q(t + 1)

        @pl.when(t + 1 == nz)
        def _():
            len_copy.wait_recv()
            kv[0].wait_recv()
            set_bias(1, plen[0:1, :])

        @pl.when(t == nz)
        def _():
            kv[1].wait_recv()
            turn(1)

    def after(t):
        @pl.when(t >= nz)
        def _():
            for off in range(1, nx):
                px_copy(t - nz, off).start()

        @pl.when(t >= nz + 1)
        def _():
            merge_x(t - nz - 1)
            pz_copy(t - nz - 1).start()

    need_q(0)
    m = None
    for j in range(chunks):
        m = scores(0, plane(0), s_a, j, m)
    m = fresh_scores(0, plane(0), s_a, m)

    def pair(i, m):
        t = 2 * i
        before(t)
        m = step(t, s_a, s_b, m, True)
        after(t)
        before(t + 1)
        m = step(t + 1, s_b, s_a, m, True)
        after(t + 1)
        return m

    m = lax.fori_loop(0, nz - 1, pair, m)
    last = 2 * nz - 2
    before(last)
    m = step(last, s_a, s_b, m, True)
    after(last)
    step(last + 1, s_b, s_a, m, False)
    after(last + 1)

    merge_x(nz - 1)
    tiles, blocks = [zpart[z, 128:136, :]], [zpart[z, 0:128, :]]
    for t in range(nz - 1):
        pz_arrival(t).wait_recv()
        tiles.append(zin[t, 128:136, :])
        blocks.append(zin[t, 0:128, :])
    peak, total, value = merged(tiles, blocks)
    fout[...] = (value / total).T.astype(jnp.bfloat16)

    def home(off):
        w, h_, y_ = col_peer(off)
        src = fout.at[pl.ds(pl.multiple_of(w * 16, 16), 16), :]
        return remote(src, fin.at[NY * h + y], f_s.at[w], f_r.at[u], at(h_, x, y_, z))

    def home_arrival(off):
        w, h_, y_ = col_peer(off)
        src = fout.at[pl.ds(0, 16), :]
        return remote(src, fin.at[NY * h_ + y_], f_s.at[w], f_r.at[w], at(h_, x, y_, z))

    for off in range(1, COL):
        home(off).start()
    fin[NY * h + y] = fout[pl.ds(pl.multiple_of(u * 16, 16), 16), :]
    for off in range(1, COL):
        home_arrival(off).wait_recv()
    out[...] = fin[...]

    for off in range(1, COL):
        col_copy(off).wait_send()
        home(off).wait_send()
    len_copy.wait_send()
    for copy in kv:
        copy.wait_send()
    for t in range(nz):
        for off in range(1, nx):
            qx_copy(t, off).wait_send()
            px_copy(t, off).wait_send()
        if t < nz - 1:
            qz_copy(t).wait_send()
            pz_copy(t).wait_send()


def shards(nx, nz, q_new, kv_new, k_cache, v_cache, span_len, order):
    kv_dev, slots, width = k_cache.shape
    tokens = q_new.shape[0]
    kv_heads = NH * kv_dev
    group = q_new.shape[1] // (kv_heads * width)
    rows = 128 * nx
    bf = jnp.bfloat16
    queries = q_new.reshape(tokens, kv_heads, group, width).transpose(1, 0, 2, 3)
    queries = queries.reshape(kv_heads, tokens * group, width)
    fresh = kv_new.reshape(tokens, kv_heads, 2, width).transpose(1, 2, 0, 3)
    fresh = fresh.reshape(kv_heads, 2 * tokens, width)
    pad = jnp.zeros((kv_heads, 16 - 2 * tokens, width), bf)
    msg = jnp.concatenate([queries, fresh, pad], axis=1)
    grid = order.astype(jnp.float32).reshape(NH, nx, NY, nz, tokens).transpose(3, 1, 2, 0, 4)
    grid = jnp.broadcast_to(grid.reshape(nz, 1, rows // group, 1), (nz, 8, rows // group, group))
    ordq = grid.reshape(nz, 8, rows)
    lens = jnp.broadcast_to(span_len.astype(jnp.float32).reshape(1, 1), (8, 128))
    scale2 = width ** (-0.5) * 1.4426950408889634
    vmem = pl.BlockSpec(memory_space=pltpu.VMEM)
    hbm = pl.BlockSpec(memory_space=pltpu.HBM)
    f32 = jnp.float32
    dma = pltpu.SemaphoreType.DMA
    out = pl.pallas_call(
        functools.partial(kernel, nx, nz, scale2),
        out_shape=jax.ShapeDtypeStruct((kv_heads, tokens * group, width), bf),
        in_specs=[vmem, vmem, vmem, hbm, hbm],
        out_specs=vmem,
        scratch_shapes=[
            pltpu.VMEM((COL, 32, width), bf),
            pltpu.VMEM((nz, rows, width), bf),
            pltpu.VMEM((2, slots, width), bf),
            pltpu.VMEM((2, slots, width), bf),
            pltpu.VMEM((2, width, slots), bf),
            pltpu.VMEM((2, 16, width), bf),
            pltpu.VMEM((2, 16, width), bf),
            pltpu.VMEM((2, 16, width), f32),
            pltpu.VMEM((2, slots, 128), f32),
            pltpu.VMEM((8, 128), f32),
            pltpu.VMEM((slots + 8, rows), f32),
            pltpu.VMEM((slots + 8, rows), f32),
            pltpu.VMEM((width, rows), f32),
            pltpu.VMEM((nz, nx, width + 8, 128), f32),
            pltpu.VMEM((nz, nx, width + 8, 128), f32),
            pltpu.VMEM((nz, width + 8, 128), f32),
            pltpu.VMEM((nz, width + 8, 128), f32),
            pltpu.VMEM((kv_heads, 16, width), bf),
            pltpu.VMEM((128, width), bf),
            dma((COL,)), dma((COL,)), dma, dma, dma((2,)), dma((2,)), dma((2,)),
            dma((nz,)), dma((nz,)), dma((nz, nx)), dma((nz, nx)),
            dma((nz, nx)), dma((nz, nx)), dma((nz,)), dma((nz,)), dma((COL,)), dma((COL,)),
        ],
        compiler_params=pltpu.CompilerParams(
            collective_id=0, has_side_effects=True, vmem_limit_bytes=48 << 20
        ),
    )(msg, ordq, lens, k_cache, v_cache)
    out = out.reshape(kv_heads, tokens, group, width).transpose(1, 0, 2, 3)
    return out.reshape(tokens, kv_heads * group * width)


def solution(mesh):
    nz = 8
    nx = mesh.shape["ctx"] // (nz * NY)
    return jax.shard_map(
        functools.partial(shards, nx, nz),
        mesh=mesh,
        in_specs=(
            P(("head", "ctx"), None),
            P(("head", "ctx"), None),
            P("head", "ctx", None),
            P("head", "ctx", None),
            P("ctx"),
            P(),
        ),
        out_specs=P(("head", "ctx"), None),
        check_vma=False,
    )
```

```python
import functools

import jax
import jax.numpy as jnp
from jax import lax
from jax.experimental import pallas as pl
from jax.experimental.pallas import tpu as pltpu
from jax.sharding import PartitionSpec as P

MESH = pl.DeviceIdType.MESH
masked = -1e30
NH = 4
NY = 2
COL = NH * NY
CHUNK = 256


def kernel(
    nx, nz, scale2,
    q_hbm, f_hbm, len_smem, ord_hbm, k_hbm, v_hbm,
    out,
    q_in, f_in, ord_in, msg, ordq, lens,
    col, qall, kb, vb, vt, kf, vf, fresh_f, bias, plen, s_a, s_b, acc, part,
    xout, xin, zout, zin, fin, fout,
    col_s, col_r, len_s, len_r, kv_s, kv_r, own_sem, qz_s, qz_r, qx_s, qx_r,
    px_s, px_r, pz_s, pz_r, f_s, f_r,
):
    h = lax.axis_index("head")
    c = lax.axis_index("ctx")
    z = lax.rem(c, nz)
    y = lax.rem(lax.div(c, nz), NY)
    x = lax.div(c, nz * NY)
    u = y * NH + h
    slots = k_hbm.shape[1]
    rows = 128 * nx
    chunks = slots // CHUNK

    def at(h_, x_, y_, z_):
        return (h_, (x_ * NY + y_) * nz + z_)

    def col_peer(off):
        w = lax.rem(u + off, COL)
        return w, lax.rem(w, NH), lax.div(w, NH)

    def remote(src, dst, ss, rs, dev):
        return pltpu.make_async_remote_copy(
            src_ref=src, dst_ref=dst, send_sem=ss, recv_sem=rs, device_id=dev, device_id_type=MESH
        )

    def far(t):
        half = lax.div(t, 2)
        return jnp.where(lax.rem(t, 2) == 0, nz // 2 + half, nz // 2 - 1 - half)

    def plane(t):
        return lax.rem(z + far(t), nz)

    own = [
        pltpu.make_async_copy(k_hbm.at[y], kb.at[0], own_sem.at[0]),
        pltpu.make_async_copy(v_hbm.at[y], vb.at[0], own_sem.at[1]),
    ]
    small = [
        pltpu.make_async_copy(q_hbm, q_in, own_sem.at[2]),
        pltpu.make_async_copy(f_hbm, f_in, own_sem.at[3]),
        pltpu.make_async_copy(ord_hbm, ord_in, own_sem.at[4]),
    ]
    for copy in small + own:
        copy.start()

    barrier = pltpu.get_barrier_semaphore()
    for off in range(1, COL):
        _, h_, y_ = col_peer(off)
        pl.semaphore_signal(barrier, inc=1, device_id=at(h_, x, y_, z), device_id_type=MESH)
    for off in range(1, nz):
        pl.semaphore_signal(
            barrier, inc=1, device_id=at(h, x, y, lax.rem(z + off, nz)), device_id_type=MESH
        )
    for off in range(1, nx):
        pl.semaphore_signal(
            barrier, inc=1, device_id=at(h, lax.rem(x + off, nx), y, z), device_id_type=MESH
        )

    tile_row = lax.broadcasted_iota(jnp.int32, (8, 128), 0)
    pair_row = lax.broadcasted_iota(jnp.int32, (16, 128), 0)
    lens[...] = jnp.zeros((8, 128), jnp.float32) + len_smem[0].astype(jnp.float32)

    def set_bias(span, length):
        for j in range(chunks):
            slot = lax.broadcasted_iota(jnp.int32, (CHUNK, 128), 0).astype(jnp.float32) + j * CHUNK
            bias[span, j * CHUNK : (j + 1) * CHUNK, :] = jnp.where(slot < length, 0.0, masked)

    set_bias(0, lens[0:1, :])
    for d in range(nz):
        for w in range(nx):
            part[d, w, 0:128, :] = jnp.zeros((128, 128), jnp.float32)
            part[d, w, 128:136, :] = jnp.where(tile_row == 0, masked, 0.0)
    for copy in small:
        copy.wait()
    for w in range(COL):
        msg[w, 0:16, :] = q_in[w * 16 : (w + 1) * 16, :]
        msg[w, 16:32, :] = f_in[w // 4 * 16 : w // 4 * 16 + 16, :]

    places = ord_in.shape[1]
    pos = ord_in[...]
    high, low = lax.div(pos, 16), lax.rem(pos, 16)
    digits = jnp.concatenate([high, low], axis=0).astype(jnp.float32).astype(jnp.bfloat16)
    lane = lax.broadcasted_iota(jnp.int32, (places, rows), 1)
    place = lax.broadcasted_iota(jnp.int32, (places, rows), 0)
    source = lax.div(lane, 64) * (2 * nz) + lax.rem(lane, 2)
    lane8 = lax.broadcasted_iota(jnp.int32, (8, rows), 1)
    picked = lax.rem(lax.div(lane8, 16), NH) == lax.rem(lax.broadcasted_iota(jnp.int32, (8, rows), 0), NH)
    for d in range(nz):
        pick = jnp.where(place == source + 2 * d, 1.0, 0.0).astype(jnp.bfloat16)
        both = jnp.dot(digits, pick, preferred_element_type=jnp.float32)
        both = jnp.where(picked, both, 0.0) * jnp.where(
            lax.broadcasted_iota(jnp.int32, (8, rows), 0) < NH, 16.0, 1.0
        )
        ordq[d] = jnp.broadcast_to(jnp.sum(both, axis=0, keepdims=True), (8, rows))

    pl.semaphore_wait(barrier, COL + nz + nx - 3)

    def col_copy(off):
        w, h_, y_ = col_peer(off)
        return remote(
            msg.at[NY * h_ + y_], col.at[u], col_s.at[w], col_r.at[u], at(h_, x, y_, z)
        )

    def col_arrival(off):
        w, h_, y_ = col_peer(off)
        return remote(msg.at[0], col.at[w], col_s.at[w], col_r.at[w], at(h_, x, y_, z))

    for off in range(1, COL):
        col_copy(off).start()
    partner = at(h, x, 1 - y, z)
    len_copy = remote(lens, plen, len_s, len_r, partner)
    len_copy.start()
    kv = [
        remote(k_hbm.at[1 - y], kb.at[1], kv_s.at[0], kv_r.at[0], partner),
        remote(v_hbm.at[1 - y], vb.at[1], kv_s.at[1], kv_r.at[1], partner),
    ]
    for copy in kv:
        copy.start()
    col[u] = msg[NY * h + y]

    def turn(span):
        for j in range(slots // 128):
            vt[span, :, j * 128 : (j + 1) * 128] = vb[span, j * 128 : (j + 1) * 128, :].T

    for copy in own:
        copy.wait()
    turn(0)
    for off in range(1, COL):
        col_arrival(off).wait_recv()

    base = pl.multiple_of(x * 128, 128)
    for w in range(COL):
        qall[z, pl.ds(pl.multiple_of(x * 128 + w * 16, 16), 16), :] = col[w, 0:16, :]

    def qz_copy(t):
        to = lax.rem(z + nz - far(t), nz)
        ref = qall.at[z, pl.ds(base, 128), :]
        return remote(ref, ref, qz_s.at[t], qz_r.at[t], at(h, x, y, to))

    def qz_arrival(t):
        ref = qall.at[plane(t), pl.ds(base, 128), :]
        return remote(ref, ref, qz_s.at[t], qz_r.at[t], at(h, x, y, plane(t)))

    def qx_copy(t, off):
        ref = qall.at[plane(t), pl.ds(base, 128), :]
        return remote(
            ref, ref, qx_s.at[t, off], qx_r.at[t, off], at(h, lax.rem(x + off, nx), y, z)
        )

    def qx_arrival(t, off):
        who = lax.rem(x + nx - off, nx)
        ref = qall.at[plane(t), pl.ds(pl.multiple_of(who * 128, 128), 128), :]
        return remote(ref, ref, qx_s.at[t, off], qx_r.at[t, off], at(h, who, y, z))

    for off in range(1, nx):
        qx_copy(nz - 1, off).start()
    for k in reversed(range(nz - 1)):
        qz_copy(k).start()

    for span in range(2):
        side = y if span == 0 else 1 - y
        fresh_f[1:3] = jnp.zeros((2, 16, 128), jnp.float32)
        first = 4 * lax.rem(NY * h + y, 4)
        for w in range(NH):
            fresh_f[0] = col[side * NH + w, 16:32, :].astype(jnp.float32)
            fresh_f[1, 2 * w : 2 * w + 2, :] = fresh_f[0, pl.ds(first, 2), :]
            fresh_f[2, 2 * w : 2 * w + 2, :] = fresh_f[0, pl.ds(first + 2, 2), :]
        kf[span] = fresh_f[1].astype(jnp.bfloat16)
        vf[span] = fresh_f[2].astype(jnp.bfloat16)

    mine = ordq[z, :, pl.ds(base, 128)]
    lane = lax.broadcasted_iota(jnp.int32, (8, 128), 1)

    def key_order(side):
        hit = lax.div(lane, 16) == lax.div(tile_row, 2) + NH * side
        hit = hit & (lax.rem(lane, 2) == lax.rem(tile_row, 2))
        return jnp.max(jnp.where(hit, mine, -1.0), axis=1, keepdims=True)

    fresh_order = (key_order(y), key_order(1 - y))

    def forward(k):
        qz_arrival(k).wait_recv()
        for off in range(1, nx):
            qx_copy(k, off).start()

    for t in range(1, min(3, nz)):
        forward(nz - 1 - t)

    def scores(span, d, s_ref, j, m):
        keys = kb[span, j * CHUNK : (j + 1) * CHUNK, :]
        s = lax.dot_general(
            keys, qall[d], (((1,), (1,)), ((), ())), preferred_element_type=jnp.float32
        )
        s = s + jnp.concatenate([bias[span, j * CHUNK : (j + 1) * CHUNK, :]] * nx, axis=1)
        s_ref[j * CHUNK : (j + 1) * CHUNK, :] = s
        top = jnp.max(s.reshape(CHUNK // 8, 8, rows), axis=0)
        return top if m is None else jnp.maximum(m, top)

    def fresh_scores(span, d, s_ref, m):
        s = lax.dot_general(
            kf[span], qall[d], (((1,), (1,)), ((), ())), preferred_element_type=jnp.float32
        )
        key = jnp.where(span == 0, fresh_order[0], fresh_order[1])
        s = jnp.where(key <= ordq[d], s[0:8, :], masked)
        s_ref[slots : slots + 8, :] = s
        return jnp.maximum(m, s)

    def weights(span, s_ref, j, peak, total):
        p = jnp.exp2(s_ref[j * CHUNK : (j + 1) * CHUNK, :] * scale2 - peak)
        total = total + jnp.sum(p.reshape(CHUNK // 8, 8, rows), axis=0)
        values = vt[span, :, j * CHUNK : (j + 1) * CHUNK]
        more = jnp.dot(values, p.astype(jnp.bfloat16), preferred_element_type=jnp.float32)
        if j == 0:
            acc[...] = more
        else:
            acc[...] += more
        return total

    def fresh_weights(span, s_ref, peak, total):
        p = jnp.exp2(s_ref[slots : slots + 8, :] * scale2 - peak)
        both = jnp.concatenate([p, jnp.zeros_like(p)], axis=0).astype(jnp.bfloat16)
        acc[...] += lax.dot_general(
            vf[span], both, (((0,), (0,)), ((), ())), preferred_element_type=jnp.float32
        )
        return total + p

    def add_part(d, peak, total):
        total = jnp.sum(total, axis=0, keepdims=True)
        for w in range(nx):
            cut = slice(w * 128, (w + 1) * 128)
            old = part[d, w, 128:136, :]
            new_peak = jnp.maximum(old[0:1, :], peak[:, cut])
            keep = jnp.exp2(old[0:1, :] - new_peak)
            take = jnp.exp2(peak[:, cut] - new_peak)
            part[d, w, 0:128, :] = part[d, w, 0:128, :] * keep + acc[:, cut] * take
            new_total = old[1:2, :] * keep + total[:, cut] * take
            part[d, w, 128:136, :] = jnp.where(tile_row == 0, new_peak, new_total)

    def order_of(t):
        return jnp.where(t < nz, nz - 1 - t, t - nz)

    def step(t, s_now, s_next, m, ahead):
        span, d = lax.div(t, nz), plane(order_of(t))
        span_n, d_n = lax.div(t + 1, nz), plane(order_of(t + 1))
        peak = jnp.max(m, axis=0, keepdims=True) * scale2
        total = jnp.zeros((8, rows), jnp.float32)
        nxt = None
        for j in range(chunks):
            if ahead:
                nxt = scores(span_n, d_n, s_next, j, nxt)
            total = weights(span, s_now, j, peak, total)
        if ahead:
            nxt = fresh_scores(span_n, d_n, s_next, nxt)
        total = fresh_weights(span, s_now, peak, total)
        add_part(d, peak, total)
        return nxt

    def encode(ref, value, peak, total, peak_total):
        size = jnp.maximum(jnp.max(jnp.abs(value), axis=0, keepdims=True), 1e-30)
        power = jnp.ceil(jnp.log2(size) + peak + 1e-3) - 15.0
        power_t = jnp.ceil(jnp.log2(total) + peak_total + 1e-3) - 15.0
        units = value * jnp.exp2(peak - power)
        units = (units + 12582912.0) - 12582912.0
        whole = total * jnp.exp2(peak_total - power_t)
        high = jnp.floor(whole)
        low = jnp.floor((whole - high) * 32767.0)
        tail = jnp.where(pair_row == 0, power, jnp.where(pair_row == 1, power_t, high))
        tail = jnp.where(pair_row == 3, low, tail)
        ref[0:128, :] = units.astype(jnp.int32).astype(jnp.int16)
        ref[128:144, :] = tail.astype(jnp.int32).astype(jnp.int16)

    def decode(ref):
        tail = ref[128:144, :].astype(jnp.int32).astype(jnp.float32)
        total = tail[2:3, :] + tail[3:4, :] * (1.0 / 32767.0)
        return ref[0:128, :].astype(jnp.int32).astype(jnp.float32), tail[0:1, :], total, tail[1:2, :]

    def merged(items):
        peak = functools.reduce(jnp.maximum, [item[1] for item in items])
        peak_total = functools.reduce(jnp.maximum, [item[3] for item in items])
        value = sum(item[0] * jnp.exp2(item[1] - peak) for item in items)
        total = sum(item[2] * jnp.exp2(item[3] - peak_total) for item in items)
        return value, peak, total, peak_total

    def px_copy(k, off):
        who = lax.rem(x + off, nx)
        return remote(xout.at[k, off], xin.at[k, off], px_s.at[k, off], px_r.at[k, off], at(h, who, y, z))

    def px_arrival(k, off):
        who = lax.rem(x + nx - off, nx)
        return remote(xout.at[k, off], xin.at[k, off], px_s.at[k, off], px_r.at[k, off], at(h, who, y, z))

    def pz_copy(k):
        return remote(zout.at[k], zin.at[k], pz_s.at[k], pz_r.at[k], at(h, x, y, plane(k)))

    def pz_arrival(k):
        who = lax.rem(z + nz - far(k), nz)
        return remote(zout.at[k], zin.at[k], pz_s.at[k], pz_r.at[k], at(h, x, y, who))

    def send_x(k):
        d = plane(k)
        for off in range(1, nx):
            who = lax.rem(x + off, nx)
            tile = part[d, who, 128:136, :]
            encode(xout.at[k, off], part[d, who, 0:128, :], tile[0:1, :], tile[1:2, :], tile[0:1, :])
            px_copy(k, off).start()

    def merge_x(k):
        tile = part[plane(k), x, 128:136, :]
        items = [(part[plane(k), x, 0:128, :], tile[0:1, :], tile[1:2, :], tile[0:1, :])]
        for off in range(1, nx):
            px_arrival(k, off).wait_recv()
            items.append(decode(xin.at[k, off]))
        return merged(items)

    def send_z(k):
        encode(zout.at[k], *merge_x(k))
        pz_copy(k).start()

    def need_q(t):
        for off in range(1, nx):
            qx_arrival(nz - 1 - t, off).wait_recv()

    def before(t):
        @pl.when(t + 3 < nz)
        def _():
            forward(nz - 4 - t)

        @pl.when(t + 1 < nz)
        def _():
            need_q(t + 1)

        @pl.when(t + 1 == nz)
        def _():
            len_copy.wait_recv()
            kv[0].wait_recv()
            set_bias(1, plen[0:1, :])

        @pl.when(t == nz)
        def _():
            kv[1].wait_recv()
            turn(1)

    def after(t):
        @pl.when(t >= nz)
        def _():
            send_x(t - nz)

        @pl.when(t >= nz + 1)
        def _():
            send_z(t - nz - 1)

    need_q(0)
    m = None
    for j in range(chunks):
        m = scores(0, z, s_a, j, m)
    m = fresh_scores(0, z, s_a, m)

    def pair(i, m):
        t = 2 * i
        before(t)
        m = step(t, s_a, s_b, m, True)
        after(t)
        before(t + 1)
        m = step(t + 1, s_b, s_a, m, True)
        after(t + 1)
        return m

    m = lax.fori_loop(0, nz - 1, pair, m)
    last = 2 * nz - 2
    before(last)
    m = step(last, s_a, s_b, m, True)
    after(last)
    step(last + 1, s_b, s_a, m, False)
    after(last + 1)

    items = [merge_x(nz - 1)]
    for k in range(nz - 1):
        pz_arrival(k).wait_recv()
        items.append(decode(zin.at[k]))
    value, peak, total, peak_total = merged(items)
    value = value * (jnp.exp2(peak - peak_total) / total)
    fout[...] = value.T.astype(jnp.bfloat16)

    def home(off):
        w, h_, y_ = col_peer(off)
        src = fout.at[pl.ds(pl.multiple_of(w * 16, 16), 16), :]
        return remote(src, fin.at[NY * h + y], f_s.at[w], f_r.at[u], at(h_, x, y_, z))

    def home_arrival(off):
        w, h_, y_ = col_peer(off)
        src = fout.at[pl.ds(0, 16), :]
        return remote(src, fin.at[NY * h_ + y_], f_s.at[w], f_r.at[w], at(h_, x, y_, z))

    for off in range(1, COL):
        home(off).start()
    fin[NY * h + y] = fout[pl.ds(pl.multiple_of(u * 16, 16), 16), :]
    for off in range(1, COL):
        home_arrival(off).wait_recv()
    out[...] = fin[...]

    for off in range(1, COL):
        col_copy(off).wait_send()
        home(off).wait_send()
    len_copy.wait_send()
    for copy in kv:
        copy.wait_send()
    for t in range(nz):
        for off in range(1, nx):
            qx_copy(t, off).wait_send()
            px_copy(t, off).wait_send()
        if t < nz - 1:
            qz_copy(t).wait_send()
            pz_copy(t).wait_send()


def shards(nx, nz, q_new, kv_new, k_cache, v_cache, span_len, order):
    kv_dev, slots, width = k_cache.shape
    tokens = q_new.shape[0]
    kv_heads = NH * kv_dev
    group = q_new.shape[1] // (kv_heads * width)
    rows = 128 * nx
    bf = jnp.bfloat16
    queries = q_new.reshape(tokens, kv_heads * group, width).transpose(1, 0, 2)
    queries = queries.reshape(kv_heads * group * tokens, width)
    fresh = kv_new.reshape(tokens, kv_heads * 2, width).transpose(1, 0, 2)
    fresh = fresh.reshape(kv_heads * 2 * tokens, width)
    places = order.reshape(NH, -1)
    scale2 = width ** (-0.5) * 1.4426950408889634
    vmem = pl.BlockSpec(memory_space=pltpu.VMEM)
    hbm = pl.BlockSpec(memory_space=pltpu.HBM)
    smem = pl.BlockSpec(memory_space=pltpu.SMEM)
    i16 = jnp.int16
    f32 = jnp.float32
    dma = pltpu.SemaphoreType.DMA
    out = pl.pallas_call(
        functools.partial(kernel, nx, nz, scale2),
        out_shape=jax.ShapeDtypeStruct((kv_heads, tokens * group, width), bf),
        in_specs=[hbm, hbm, smem, hbm, hbm, hbm],
        out_specs=vmem,
        scratch_shapes=[
            pltpu.VMEM(queries.shape, bf),
            pltpu.VMEM(fresh.shape, bf),
            pltpu.VMEM(places.shape, jnp.int32),
            pltpu.VMEM((COL, 32, width), bf),
            pltpu.VMEM((nz, 8, rows), f32),
            pltpu.VMEM((8, 128), f32),
            pltpu.VMEM((COL, 32, width), bf),
            pltpu.VMEM((nz, rows, width), bf),
            pltpu.VMEM((2, slots, width), bf),
            pltpu.VMEM((2, slots, width), bf),
            pltpu.VMEM((2, width, slots), bf),
            pltpu.VMEM((2, 16, width), bf),
            pltpu.VMEM((2, 16, width), bf),
            pltpu.VMEM((3, 16, width), f32),
            pltpu.VMEM((2, slots, 128), f32),
            pltpu.VMEM((8, 128), f32),
            pltpu.VMEM((slots + 8, rows), f32),
            pltpu.VMEM((slots + 8, rows), f32),
            pltpu.VMEM((width, rows), f32),
            pltpu.VMEM((nz, nx, width + 8, 128), f32),
            pltpu.VMEM((nz, nx, width + 16, 128), i16),
            pltpu.VMEM((nz, nx, width + 16, 128), i16),
            pltpu.VMEM((nz, width + 16, 128), i16),
            pltpu.VMEM((nz, width + 16, 128), i16),
            pltpu.VMEM((kv_heads, 16, width), bf),
            pltpu.VMEM((128, width), bf),
            dma((COL,)), dma((COL,)), dma, dma, dma((2,)), dma((2,)), dma((5,)),
            dma((nz,)), dma((nz,)), dma((nz, nx)), dma((nz, nx)),
            dma((nz, nx)), dma((nz, nx)), dma((nz,)), dma((nz,)), dma((COL,)), dma((COL,)),
        ],
        compiler_params=pltpu.CompilerParams(
            collective_id=0, has_side_effects=True, vmem_limit_bytes=62 << 20
        ),
    )(queries, fresh, span_len, places, k_cache, v_cache)
    out = out.reshape(kv_heads * group, tokens, width).transpose(1, 0, 2)
    return out.reshape(tokens, kv_heads * group * width)


def solution(mesh):
    nz = 8
    nx = mesh.shape["ctx"] // (nz * NY)
    return jax.shard_map(
        functools.partial(shards, nx, nz),
        mesh=mesh,
        in_specs=(
            P(("head", "ctx"), None),
            P(("head", "ctx"), None),
            P("head", "ctx", None),
            P("head", "ctx", None),
            P("ctx"),
            P(),
        ),
        out_specs=P(("head", "ctx"), None),
        check_vma=False,
    )
```

```python
import functools

import jax
import jax.numpy as jnp
from jax import lax
from jax.experimental import pallas as pl
from jax.experimental.pallas import tpu as pltpu
from jax.sharding import PartitionSpec as P

MESH = pl.DeviceIdType.MESH
masked = -1e30
NH = 4
NY = 2
COL = NH * NY
CHUNK = 256
LAG = 3


def kernel(
    nx, nz, scale2,
    q_hbm, f_hbm, len_hbm, ord_hbm, k_hbm, v_hbm,
    out,
    q_in, f_in, ord_in, len_smem, msg, ordq, lens,
    col, qall, kb, vb, vt, vo, kf, vf, fresh_f, bias, plen, s_a, s_b, acc, part,
    xout, xin, zfull, zout, zin, fout,
    col_s, col_r, len_s, len_r, kv_s, kv_r, own_sem, qz_s, qz_r, qx_s, qx_r,
    px_s, px_r, pz_s, pz_r, f_s, f_r,
):
    h = lax.axis_index("head")
    c = lax.axis_index("ctx")
    z = lax.rem(c, nz)
    y = lax.rem(lax.div(c, nz), NY)
    x = lax.div(c, nz * NY)
    u = y * NH + h
    slots = k_hbm.shape[1]
    rows = 128 * nx
    width = k_hbm.shape[2]
    chunks = slots // CHUNK

    def at(h_, x_, y_, z_):
        return (h_, (x_ * NY + y_) * nz + z_)

    def col_peer(off):
        w = lax.rem(u + off, COL)
        return w, lax.rem(w, NH), lax.div(w, NH)

    def remote(src, dst, ss, rs, dev):
        return pltpu.make_async_remote_copy(
            src_ref=src, dst_ref=dst, send_sem=ss, recv_sem=rs, device_id=dev, device_id_type=MESH
        )

    def far(k):
        half = lax.div(k - 2, 2)
        rest = jnp.where(lax.rem(k, 2) == 0, nz // 2 + half, nz // 2 - 1 - half)
        return jnp.where(k == 0, 1, jnp.where(k == 1, nz - 1, jnp.where(k == nz - 1, 0, rest)))

    def plane(t):
        return lax.rem(z + far(t), nz)

    own = [
        pltpu.make_async_copy(k_hbm.at[y], kb.at[0], own_sem.at[0]),
        pltpu.make_async_copy(v_hbm, vb, own_sem.at[1]),
    ]
    small = [
        pltpu.make_async_copy(q_hbm, q_in, own_sem.at[2]),
        pltpu.make_async_copy(f_hbm, f_in, own_sem.at[3]),
        pltpu.make_async_copy(ord_hbm, ord_in, own_sem.at[4]),
        pltpu.make_async_copy(len_hbm, len_smem, own_sem.at[5]),
    ]
    for copy in small + own:
        copy.start()

    barrier = pltpu.get_barrier_semaphore()
    for off in range(1, COL):
        _, h_, y_ = col_peer(off)
        pl.semaphore_signal(barrier, inc=1, device_id=at(h_, x, y_, z), device_id_type=MESH)
    for off in range(1, nz):
        pl.semaphore_signal(
            barrier, inc=1, device_id=at(h, x, y, lax.rem(z + off, nz)), device_id_type=MESH
        )
    for off in range(1, nx):
        for side in (0, 1, nz - 1):
            to = at(h, lax.rem(x + off, nx), y, lax.rem(z + side, nz))
            pl.semaphore_signal(barrier, inc=1, device_id=to, device_id_type=MESH)

    tile_row = lax.broadcasted_iota(jnp.int32, (8, 128), 0)
    wide_row = lax.broadcasted_iota(jnp.int32, (8, rows), 0)
    for copy in small:
        copy.wait()
    lens[...] = jnp.zeros((8, 128), jnp.float32) + len_smem[0].astype(jnp.float32)

    def set_bias(span, length):
        for j in range(chunks):
            slot = lax.broadcasted_iota(jnp.int32, (CHUNK, 128), 0).astype(jnp.float32) + j * CHUNK
            bias[span, j * CHUNK : (j + 1) * CHUNK, :] = jnp.where(slot < length, 0.0, masked)

    set_bias(0, lens[0:1, :])
    for w in range(COL):
        msg[w, 0:16, :] = q_in[w * 16 : (w + 1) * 16, :]
        msg[w, 16:32, :] = f_in[w // 4 * 16 : w // 4 * 16 + 16, :]

    places = ord_in.shape[1]
    pos = ord_in[...]
    high, low = lax.div(pos, 16), lax.rem(pos, 16)
    digits = jnp.concatenate([high, low], axis=0).astype(jnp.float32).astype(jnp.bfloat16)
    lane = lax.broadcasted_iota(jnp.int32, (places, rows), 1)
    place = lax.broadcasted_iota(jnp.int32, (places, rows), 0)
    source = lax.div(lane, 64) * (2 * nz) + lax.rem(lane, 2)
    lane8 = lax.broadcasted_iota(jnp.int32, (8, rows), 1)
    picked = lax.rem(lax.div(lane8, 16), NH) == lax.rem(lax.broadcasted_iota(jnp.int32, (8, rows), 0), NH)
    for d in range(nz):
        pick = jnp.where(place == source + 2 * d, 1.0, 0.0).astype(jnp.bfloat16)
        both = jnp.dot(digits, pick, preferred_element_type=jnp.float32)
        both = jnp.where(picked, both, 0.0) * jnp.where(
            lax.broadcasted_iota(jnp.int32, (8, rows), 0) < NH, 16.0, 1.0
        )
        ordq[d] = jnp.broadcast_to(jnp.sum(both, axis=0, keepdims=True), (8, rows))

    for copy in own:
        copy.wait()
    for j in range(slots // 128):
        cut = slice(j * 128, (j + 1) * 128)
        vt[0, :, cut] = vb[y, cut, :].T
        vo[:, cut] = vb[1 - y, cut, :].T

    pl.semaphore_wait(barrier, COL + nz - 2 + 3 * (nx - 1))

    def col_copy(off):
        w, h_, y_ = col_peer(off)
        return remote(
            msg.at[NY * h_ + y_], col.at[u], col_s.at[w], col_r.at[u], at(h_, x, y_, z)
        )

    def col_arrival(off):
        w, h_, y_ = col_peer(off)
        return remote(msg.at[0], col.at[w], col_s.at[w], col_r.at[w], at(h_, x, y_, z))

    for off in range(1, COL):
        col_copy(off).start()
    partner = at(h, x, 1 - y, z)
    len_copy = remote(lens, plen, len_s, len_r, partner)
    len_copy.start()
    kv = [
        remote(k_hbm.at[1 - y], kb.at[1], kv_s.at[0], kv_r.at[0], partner),
        remote(vo, vt.at[1], kv_s.at[1], kv_r.at[1], partner),
    ]
    for copy in kv:
        copy.start()
    col[u] = msg[NY * h + y]

    for off in range(1, COL):
        col_arrival(off).wait_recv()

    base = pl.multiple_of(x * 128, 128)
    for w in range(COL):
        qall[z, pl.ds(pl.multiple_of(x * 128 + w * 16, 16), 16), :] = col[w, 0:16, :]

    def qz_copy(t):
        to = lax.rem(z + nz - far(t), nz)
        ref = qall.at[z, pl.ds(base, 128), :]
        return remote(ref, ref, qz_s.at[t], qz_r.at[t], at(h, x, y, to))

    def qd_copy(k, off):
        to = lax.rem(z + nz - far(k), nz)
        ref = qall.at[z, pl.ds(base, 128), :]
        return remote(ref, ref, qx_s.at[k, off], qx_r.at[k, off], at(h, lax.rem(x + off, nx), y, to))

    def qz_arrival(t):
        ref = qall.at[plane(t), pl.ds(base, 128), :]
        return remote(ref, ref, qz_s.at[t], qz_r.at[t], at(h, x, y, plane(t)))

    def qx_copy(t, off):
        ref = qall.at[plane(t), pl.ds(base, 128), :]
        return remote(
            ref, ref, qx_s.at[t, off], qx_r.at[t, off], at(h, lax.rem(x + off, nx), y, z)
        )

    def qx_arrival(t, off):
        who = lax.rem(x + nx - off, nx)
        ref = qall.at[plane(t), pl.ds(pl.multiple_of(who * 128, 128), 128), :]
        return remote(ref, ref, qx_s.at[t, off], qx_r.at[t, off], at(h, who, y, z))

    for off in range(1, nx):
        qx_copy(nz - 1, off).start()
    for k in range(2):
        for off in range(nx):
            qd_copy(k, off).start()
    for k in reversed(range(2, nz - 1)):
        qz_copy(k).start()

    for span in range(2):
        side = y if span == 0 else 1 - y
        fresh_f[1:3] = jnp.zeros((2, 16, 128), jnp.float32)
        first = 4 * lax.rem(NY * h + y, 4)
        for w in range(NH):
            fresh_f[0] = col[side * NH + w, 16:32, :].astype(jnp.float32)
            fresh_f[1, 2 * w : 2 * w + 2, :] = fresh_f[0, pl.ds(first, 2), :]
            fresh_f[2, 2 * w : 2 * w + 2, :] = fresh_f[0, pl.ds(first + 2, 2), :]
        kf[span] = fresh_f[1].astype(jnp.bfloat16)
        vf[span] = fresh_f[2].astype(jnp.bfloat16)

    mine = ordq[z, :, pl.ds(base, 128)]
    lane = lax.broadcasted_iota(jnp.int32, (8, 128), 1)

    def key_order(side):
        hit = lax.div(lane, 16) == lax.div(tile_row, 2) + NH * side
        hit = hit & (lax.rem(lane, 2) == lax.rem(tile_row, 2))
        return jnp.max(jnp.where(hit, mine, -1.0), axis=1, keepdims=True)

    fresh_order = (key_order(y), key_order(1 - y))

    def forward(k):
        qz_arrival(k).wait_recv()
        for off in range(1, nx):
            qx_copy(k, off).start()

    def scores(span, d, s_ref, j, m):
        keys = kb[span, j * CHUNK : (j + 1) * CHUNK, :]
        s = lax.dot_general(
            keys, qall[d], (((1,), (1,)), ((), ())), preferred_element_type=jnp.float32
        )
        s = s + jnp.concatenate([bias[span, j * CHUNK : (j + 1) * CHUNK, :]] * nx, axis=1)
        s_ref[j * CHUNK : (j + 1) * CHUNK, :] = s
        top = jnp.max(s.reshape(CHUNK // 8, 8, rows), axis=0)
        return top if m is None else jnp.maximum(m, top)

    def fresh_scores(span, d, s_ref, m):
        s = lax.dot_general(
            kf[span], qall[d], (((1,), (1,)), ((), ())), preferred_element_type=jnp.float32
        )
        key = jnp.where(span == 0, fresh_order[0], fresh_order[1])
        s = jnp.where(key <= ordq[d], s[0:8, :], masked)
        s_ref[slots : slots + 8, :] = s
        return jnp.maximum(m, s)

    def weights(span, s_ref, j, peak, total):
        p = jnp.exp2(s_ref[j * CHUNK : (j + 1) * CHUNK, :] * scale2 - peak)
        total = total + jnp.sum(p.reshape(CHUNK // 8, 8, rows), axis=0)
        values = vt[span, :, j * CHUNK : (j + 1) * CHUNK]
        more = jnp.dot(values, p.astype(jnp.bfloat16), preferred_element_type=jnp.float32)
        if j == 0:
            acc[...] = more
        else:
            acc[...] += more
        return total

    def fresh_weights(span, s_ref, peak, total):
        p = jnp.exp2(s_ref[slots : slots + 8, :] * scale2 - peak)
        both = jnp.concatenate([p, jnp.zeros_like(p)], axis=0).astype(jnp.bfloat16)
        acc[...] += lax.dot_general(
            vf[span], both, (((0,), (0,)), ((), ())), preferred_element_type=jnp.float32
        )
        return total + p

    def keep_part(d, peak, total):
        total = jnp.sum(total, axis=0, keepdims=True)
        part[d, 0:width, :] = acc[...]
        part[d, width : width + 8, :] = jnp.where(wide_row == 0, peak, total)

    def whole_part(d, peak, total):
        total = jnp.sum(total, axis=0, keepdims=True)
        old = part[d, width : width + 8, :]
        new_peak = jnp.maximum(old[0:1, :], peak)
        keep = jnp.exp2(old[0:1, :] - new_peak)
        take = jnp.exp2(peak - new_peak)
        value = part[d, 0:width, :] * keep + acc[...] * take
        return value, new_peak, old[1:2, :] * keep + total * take, new_peak

    def encode(value, peak, total, peak_total):
        size = jnp.maximum(jnp.max(jnp.abs(value), axis=0, keepdims=True), 1e-30)
        power = jnp.ceil(jnp.log2(size) + peak + 1e-3) - 15.0
        power_t = jnp.ceil(jnp.log2(total) + peak_total + 1e-3) - 15.0
        units = value * jnp.exp2(peak - power)
        units = (units + 12582912.0) - 12582912.0
        whole = total * jnp.exp2(peak_total - power_t)
        high = jnp.floor(whole)
        low = jnp.floor((whole - high) * 32767.0)
        row = lax.broadcasted_iota(jnp.int32, (16, value.shape[1]), 0)
        tail = jnp.where(row == 0, power, jnp.where(row == 1, power_t, high))
        tail = jnp.where(row == 3, low, tail)
        both = [item.astype(jnp.int32).astype(jnp.int16) for item in (units, tail)]
        return both

    def decode(ref):
        tail = ref[width : width + 16, :].astype(jnp.int32).astype(jnp.float32)
        total = tail[2:3, :] + tail[3:4, :] * (1.0 / 32767.0)
        value = ref[0:width, :].astype(jnp.int32).astype(jnp.float32)
        return value, tail[0:1, :], total, tail[1:2, :]

    def merged(items):
        peak = functools.reduce(jnp.maximum, [item[1] for item in items])
        peak_total = functools.reduce(jnp.maximum, [item[3] for item in items])
        value = sum(item[0] * jnp.exp2(item[1] - peak) for item in items)
        total = sum(item[2] * jnp.exp2(item[3] - peak_total) for item in items)
        return value, peak, total, peak_total

    def put_part(k, item):
        units, tail = encode(*item)
        for w in range(nx):
            side = slice(w * 128, (w + 1) * 128)
            xout[k, w, 0:width, :] = units[:, side]
            xout[k, w, width : width + 16, :] = tail[:, side]

    def put_own_part(item):
        for w in range(nx):
            side = slice(w * 128, (w + 1) * 128)
            items = [tuple(array[:, side] for array in item)]
            items += [decode(zfull.at[k, w]) for k in range(2)]
            units, tail = encode(*merged(items))
            xout[nz - 1, w, 0:width, :] = units
            xout[nz - 1, w, width : width + 16, :] = tail

    def order_of(t):
        first = jnp.where(t == 0, nz - 1, jnp.where(t < 3, t - 1, nz + 1 - t))
        return jnp.where(t < nz, first, t - nz)

    def step(t, span, s_now, s_next, m, ahead=True, own_plane=False):
        k = order_of(t)
        d = plane(k)
        span_n, d_n = lax.div(t + 1, nz), plane(order_of(t + 1))
        peak = jnp.max(m, axis=0, keepdims=True) * scale2
        total = jnp.zeros((8, rows), jnp.float32)
        nxt = None
        for j in range(chunks):
            if ahead:
                nxt = scores(span_n, d_n, s_next, j, nxt)
            total = weights(span, s_now, j, peak, total)
        if ahead:
            nxt = fresh_scores(span_n, d_n, s_next, nxt)
        total = fresh_weights(span, s_now, peak, total)
        if span == 0:
            keep_part(d, peak, total)
        elif own_plane:
            for j in range(2):
                pf_arrival(j).wait_recv()
            put_own_part(whole_part(d, peak, total))
        else:
            put_part(k, whole_part(d, peak, total))
        return nxt

    def px_copy(k, off):
        who = lax.rem(x + off, nx)
        return remote(xout.at[k, who], xin.at[k, off], px_s.at[k, off], px_r.at[k, off], at(h, who, y, z))

    def px_arrival(k, off):
        who = lax.rem(x + nx - off, nx)
        return remote(xout.at[k, who], xin.at[k, off], px_s.at[k, off], px_r.at[k, off], at(h, who, y, z))

    def pf_copy(k):
        return remote(xout.at[k], zfull.at[k], pz_s.at[k], pz_r.at[k], at(h, x, y, plane(k)))

    def pf_arrival(k):
        who = lax.rem(z + nz - far(k), nz)
        return remote(xout.at[k], zfull.at[k], pz_s.at[k], pz_r.at[k], at(h, x, y, who))

    def pz_copy(k):
        return remote(zout.at[k], zin.at[k], pz_s.at[k], pz_r.at[k], at(h, x, y, plane(k)))

    def pz_arrival(k):
        who = lax.rem(z + nz - far(k), nz)
        return remote(zout.at[k], zin.at[k], pz_s.at[k], pz_r.at[k], at(h, x, y, who))

    def send_x(k):
        for off in range(1, nx):
            px_copy(k, off).start()

    def merge_x(k):
        items = [decode(xout.at[k, x])]
        for off in range(1, nx):
            px_arrival(k, off).wait_recv()
        items += [decode(xin.at[k, off]) for off in range(1, nx)]
        return merged(items)

    def send_z(k):
        units, tail = encode(*merge_x(k))
        zout[k, 0:width, :] = units
        zout[k, width : width + 16, :] = tail
        pz_copy(k).start()

    def need_x(k):
        for off in range(1, nx):
            qx_arrival(k, off).wait_recv()

    def before(t):
        @pl.when(t + 5 < nz)
        def _():
            forward(nz + 1 - (t + 5))

        @pl.when(t + 1 < nz)
        def _():
            need_x(order_of(t + 1))

        @pl.when(t + 1 < 3)
        def _():
            qx_arrival(order_of(t + 1), 0).wait_recv()

        @pl.when(t + 1 == nz)
        def _():
            len_copy.wait_recv()
            kv[0].wait_recv()
            set_bias(1, plen[0:1, :])

    def after(k):
        @pl.when(k < 2)
        def _():
            pf_copy(k).start()

        @pl.when(k >= 2)
        def _():
            send_x(k)

        @pl.when(k >= 2 + LAG)
        def _():
            send_z(k - LAG)

    need_x(nz - 1)
    m = None
    for j in range(chunks):
        m = scores(0, z, s_a, j, m)
    m = fresh_scores(0, z, s_a, m)
    for t in range(3, min(5, nz)):
        forward(nz + 1 - t)

    def pair0(i, m):
        t = 2 * i
        before(t)
        m = step(t, 0, s_a, s_b, m)
        before(t + 1)
        return step(t + 1, 0, s_b, s_a, m)

    m = lax.fori_loop(0, nz // 2, pair0, m)
    kv[1].wait_recv()

    def pair1(i, m):
        k = 2 * i
        m = step(nz + k, 1, s_a, s_b, m)
        after(k)
        m = step(nz + k + 1, 1, s_b, s_a, m)
        after(k + 1)
        return m

    m = lax.fori_loop(0, nz // 2 - 1, pair1, m)
    m = step(2 * nz - 2, 1, s_a, s_b, m)
    after(nz - 2)
    step(2 * nz - 1, 1, s_b, s_a, m, ahead=False, own_plane=True)
    after(nz - 1)
    for k in range(max(nz - LAG, 2), nz - 1):
        send_z(k)

    items = [merge_x(nz - 1)]
    for k in range(2, nz - 1):
        pz_arrival(k).wait_recv()
        items.append(decode(zin.at[k]))
    value, peak, total, peak_total = merged(items)
    value = value * (jnp.exp2(peak - peak_total) / total)
    fout[...] = value.T.astype(jnp.bfloat16)

    def home(off):
        w, h_, y_ = col_peer(off)
        src = fout.at[pl.ds(pl.multiple_of(w * 16, 16), 16), :]
        return remote(src, out.at[NY * h + y], f_s.at[w], f_r.at[u], at(h_, x, y_, z))

    def home_arrival(off):
        w, h_, y_ = col_peer(off)
        src = fout.at[pl.ds(0, 16), :]
        return remote(src, out.at[NY * h_ + y_], f_s.at[w], f_r.at[w], at(h_, x, y_, z))

    for off in range(1, COL):
        home(off).start()
    rest = pltpu.make_async_copy(
        fout.at[pl.ds(pl.multiple_of(u * 16, 16), 16), :], out.at[NY * h + y], own_sem.at[0]
    )
    rest.start()

    for off in range(1, COL):
        col_copy(off).wait_send()
    len_copy.wait_send()
    for copy in kv:
        copy.wait_send()
    for k in range(nz):
        if k >= 2:
            for off in range(1, nx):
                qx_copy(k, off).wait_send()
                px_copy(k, off).wait_send()
        if k < 2:
            for off in range(nx):
                qd_copy(k, off).wait_send()
            pf_copy(k).wait_send()
        elif k < nz - 1:
            qz_copy(k).wait_send()
            pz_copy(k).wait_send()
    for off in range(1, COL):
        home_arrival(off).wait_recv()
    rest.wait()
    for off in range(1, COL):
        home(off).wait_send()


def shards(nx, nz, q_new, kv_new, k_cache, v_cache, span_len, order):
    kv_dev, slots, width = k_cache.shape
    tokens = q_new.shape[0]
    kv_heads = NH * kv_dev
    group = q_new.shape[1] // (kv_heads * width)
    rows = 128 * nx
    bf = jnp.bfloat16
    queries = q_new.reshape(tokens, kv_heads * group, width).transpose(1, 0, 2)
    queries = queries.reshape(kv_heads * group * tokens, width)
    fresh = kv_new.reshape(tokens, kv_heads * 2, width).transpose(1, 0, 2)
    fresh = fresh.reshape(kv_heads * 2 * tokens, width)
    places = order.reshape(NH, -1)
    scale2 = width ** (-0.5) * 1.4426950408889634
    vmem = pl.BlockSpec(memory_space=pltpu.VMEM)
    hbm = pl.BlockSpec(memory_space=pltpu.HBM)
    i16 = jnp.int16
    f32 = jnp.float32
    dma = pltpu.SemaphoreType.DMA
    out = pl.pallas_call(
        functools.partial(kernel, nx, nz, scale2),
        out_shape=jax.ShapeDtypeStruct((kv_heads, tokens * group, width), bf),
        in_specs=[hbm] * 6,
        out_specs=hbm,
        scratch_shapes=[
            pltpu.VMEM(queries.shape, bf),
            pltpu.VMEM(fresh.shape, bf),
            pltpu.VMEM(places.shape, jnp.int32),
            pltpu.SMEM(span_len.shape, jnp.int32),
            pltpu.VMEM((COL, 32, width), bf),
            pltpu.VMEM((nz, 8, rows), f32),
            pltpu.VMEM((8, 128), f32),
            pltpu.VMEM((COL, 32, width), bf),
            pltpu.VMEM((nz, rows, width), bf),
            pltpu.VMEM((2, slots, width), bf),
            pltpu.VMEM((2, slots, width), bf),
            pltpu.VMEM((2, width, slots), bf),
            pltpu.VMEM((width, slots), bf),
            pltpu.VMEM((2, 16, width), bf),
            pltpu.VMEM((2, 16, width), bf),
            pltpu.VMEM((3, 16, width), f32),
            pltpu.VMEM((2, slots, 128), f32),
            pltpu.VMEM((8, 128), f32),
            pltpu.VMEM((slots + 8, rows), f32),
            pltpu.VMEM((slots + 8, rows), f32),
            pltpu.VMEM((width, rows), f32),
            pltpu.VMEM((nz, width + 8, rows), f32),
            pltpu.VMEM((nz, nx, width + 16, 128), i16),
            pltpu.VMEM((nz, nx, width + 16, 128), i16),
            pltpu.VMEM((2, nx, width + 16, 128), i16),
            pltpu.VMEM((nz, width + 16, 128), i16),
            pltpu.VMEM((nz, width + 16, 128), i16),
            pltpu.VMEM((128, width), bf),
            dma((COL,)), dma((COL,)), dma, dma, dma((2,)), dma((2,)), dma((6,)),
            dma((nz,)), dma((nz,)), dma((nz, nx)), dma((nz, nx)),
            dma((nz, nx)), dma((nz, nx)), dma((nz,)), dma((nz,)), dma((COL,)), dma((COL,)),
        ],
        compiler_params=pltpu.CompilerParams(
            collective_id=0, has_side_effects=True, vmem_limit_bytes=62 << 20
        ),
    )(queries, fresh, span_len, places, k_cache, v_cache)
    out = out.reshape(kv_heads * group, tokens, width).transpose(1, 0, 2)
    return out.reshape(tokens, kv_heads * group * width)


def solution(mesh):
    nz = 8
    nx = mesh.shape["ctx"] // (nz * NY)
    return jax.shard_map(
        functools.partial(shards, nx, nz),
        mesh=mesh,
        in_specs=(
            P(("head", "ctx"), None),
            P(("head", "ctx"), None),
            P("head", "ctx", None),
            P("head", "ctx", None),
            P("ctx"),
            P(),
        ),
        out_specs=P(("head", "ctx"), None),
        check_vma=False,
    )
```

```python
import functools

import jax
import jax.numpy as jnp
from jax import lax
from jax.experimental import pallas as pl
from jax.experimental.pallas import tpu as pltpu
from jax.sharding import PartitionSpec as P

MESH = pl.DeviceIdType.MESH
masked = -1e30
NH = 4
NY = 2
COL = NH * NY
FAR_FIRST = (2, 6, 3, 5, 1, 7, 4)
CHUNK = 256
LAG = 3


def kernel(
    nx, nz, scale2,
    q_hbm, f_hbm, len_hbm, ord_hbm, k_hbm, v_hbm,
    out,
    q_in, f_in, ord_in, len_smem, msg, ordq, lens,
    col, qall, kb, vb, vt, vo, kf, vf, fresh_f, bias, plen, s_a, s_b, acc, part,
    xout, xin, zfull, zout, zin, fout,
    col_s, col_r, len_s, len_r, kv_s, kv_r, own_sem, qz_s, qz_r, qx_s, qx_r,
    px_s, px_r, pz_s, pz_r, f_s, f_r,
):
    h = lax.axis_index("head")
    c = lax.axis_index("ctx")
    z = lax.rem(c, nz)
    y = lax.rem(lax.div(c, nz), NY)
    x = lax.div(c, nz * NY)
    u = y * NH + h
    slots = k_hbm.shape[1]
    rows = 128 * nx
    width = k_hbm.shape[2]
    chunks = slots // CHUNK

    def at(h_, x_, y_, z_):
        return (h_, (x_ * NY + y_) * nz + z_)

    def col_peer(off):
        w = lax.rem(u + off, COL)
        return w, lax.rem(w, NH), lax.div(w, NH)

    def remote(src, dst, ss, rs, dev):
        return pltpu.make_async_remote_copy(
            src_ref=src, dst_ref=dst, send_sem=ss, recv_sem=rs, device_id=dev, device_id_type=MESH
        )

    def far(k):
        half = lax.div(k - 2, 2)
        rest = jnp.where(lax.rem(k, 2) == 0, nz // 2 + half, nz // 2 - 1 - half)
        return jnp.where(k == 0, 1, jnp.where(k == 1, nz - 1, jnp.where(k == nz - 1, 0, rest)))

    def plane(t):
        return lax.rem(z + far(t), nz)

    own = [
        pltpu.make_async_copy(k_hbm.at[y], kb.at[0], own_sem.at[0]),
        pltpu.make_async_copy(v_hbm, vb, own_sem.at[1]),
    ]
    small = [
        pltpu.make_async_copy(q_hbm, q_in, own_sem.at[2]),
        pltpu.make_async_copy(f_hbm, f_in, own_sem.at[3]),
        pltpu.make_async_copy(ord_hbm, ord_in, own_sem.at[4]),
        pltpu.make_async_copy(len_hbm, len_smem, own_sem.at[5]),
    ]
    for copy in small + own:
        copy.start()

    barrier = pltpu.get_barrier_semaphore()
    for off in range(1, COL):
        _, h_, y_ = col_peer(off)
        pl.semaphore_signal(barrier, inc=1, device_id=at(h_, x, y_, z), device_id_type=MESH)
    for off in range(1, nz):
        pl.semaphore_signal(
            barrier, inc=1, device_id=at(h, x, y, lax.rem(z + off, nz)), device_id_type=MESH
        )
    for off in range(1, nx):
        pl.semaphore_signal(
            barrier, inc=1, device_id=at(h, lax.rem(x + off, nx), y, z), device_id_type=MESH
        )

    tile_row = lax.broadcasted_iota(jnp.int32, (8, 128), 0)
    wide_row = lax.broadcasted_iota(jnp.int32, (8, rows), 0)
    for copy in small:
        copy.wait()
    lens[...] = jnp.zeros((8, 128), jnp.float32) + len_smem[0].astype(jnp.float32)

    def set_bias(span, length):
        for j in range(chunks):
            slot = lax.broadcasted_iota(jnp.int32, (CHUNK, 128), 0).astype(jnp.float32) + j * CHUNK
            bias[span, j * CHUNK : (j + 1) * CHUNK, :] = jnp.where(slot < length, 0.0, masked)

    set_bias(0, lens[0:1, :])
    for w in range(COL):
        msg[w, 0:16, :] = q_in[w * 16 : (w + 1) * 16, :]
        msg[w, 16:32, :] = f_in[w // 4 * 16 : w // 4 * 16 + 16, :]

    places = ord_in.shape[1]
    pos = ord_in[...]
    high, low = lax.div(pos, 16), lax.rem(pos, 16)
    digits = jnp.concatenate([high, low], axis=0).astype(jnp.float32).astype(jnp.bfloat16)
    lane = lax.broadcasted_iota(jnp.int32, (places, rows), 1)
    place = lax.broadcasted_iota(jnp.int32, (places, rows), 0)
    source = lax.div(lane, 64) * (2 * nz) + lax.rem(lane, 2)
    lane8 = lax.broadcasted_iota(jnp.int32, (8, rows), 1)
    picked = lax.rem(lax.div(lane8, 16), NH) == lax.rem(lax.broadcasted_iota(jnp.int32, (8, rows), 0), NH)
    for d in range(nz):
        pick = jnp.where(place == source + 2 * d, 1.0, 0.0).astype(jnp.bfloat16)
        both = jnp.dot(digits, pick, preferred_element_type=jnp.float32)
        both = jnp.where(picked, both, 0.0) * jnp.where(
            lax.broadcasted_iota(jnp.int32, (8, rows), 0) < NH, 16.0, 1.0
        )
        ordq[d] = jnp.broadcast_to(jnp.sum(both, axis=0, keepdims=True), (8, rows))

    for copy in own:
        copy.wait()
    for j in range(slots // 128):
        cut = slice(j * 128, (j + 1) * 128)
        vt[0, :, cut] = vb[y, cut, :].T
        vo[:, cut] = vb[1 - y, cut, :].T

    pl.semaphore_wait(barrier, COL + nz + nx - 3)

    def col_copy(off):
        w, h_, y_ = col_peer(off)
        return remote(
            msg.at[NY * h_ + y_], col.at[u], col_s.at[w], col_r.at[u], at(h_, x, y_, z)
        )

    def col_arrival(off):
        w, h_, y_ = col_peer(off)
        return remote(msg.at[0], col.at[w], col_s.at[w], col_r.at[w], at(h_, x, y_, z))

    for off in FAR_FIRST:
        col_copy(off).start()
    partner = at(h, x, 1 - y, z)
    len_copy = remote(lens, plen, len_s, len_r, partner)
    len_copy.start()
    kv = [
        remote(k_hbm.at[1 - y], kb.at[1], kv_s.at[0], kv_r.at[0], partner),
        remote(vo, vt.at[1], kv_s.at[1], kv_r.at[1], partner),
    ]
    for copy in kv:
        copy.start()
    col[u] = msg[NY * h + y]

    for off in range(1, COL):
        col_arrival(off).wait_recv()

    base = pl.multiple_of(x * 128, 128)
    for w in range(COL):
        qall[z, pl.ds(pl.multiple_of(x * 128 + w * 16, 16), 16), :] = col[w, 0:16, :]

    def qz_copy(t):
        to = lax.rem(z + nz - far(t), nz)
        ref = qall.at[z, pl.ds(base, 128), :]
        return remote(ref, ref, qz_s.at[t], qz_r.at[t], at(h, x, y, to))

    def qf_copy(k):
        to = lax.rem(z + nz - far(k), nz)
        return remote(qall.at[z], qall.at[z], qz_s.at[k], qz_r.at[k], at(h, x, y, to))

    def qf_arrival(k):
        ref = qall.at[plane(k)]
        return remote(ref, ref, qz_s.at[k], qz_r.at[k], at(h, x, y, plane(k)))

    def qz_arrival(t):
        ref = qall.at[plane(t), pl.ds(base, 128), :]
        return remote(ref, ref, qz_s.at[t], qz_r.at[t], at(h, x, y, plane(t)))

    def qx_copy(t, off):
        ref = qall.at[plane(t), pl.ds(base, 128), :]
        return remote(
            ref, ref, qx_s.at[t, off], qx_r.at[t, off], at(h, lax.rem(x + off, nx), y, z)
        )

    def qx_arrival(t, off):
        who = lax.rem(x + nx - off, nx)
        ref = qall.at[plane(t), pl.ds(pl.multiple_of(who * 128, 128), 128), :]
        return remote(ref, ref, qx_s.at[t, off], qx_r.at[t, off], at(h, who, y, z))

    for off in range(1, nx):
        qx_copy(nz - 1, off).start()
    for k in reversed(range(2, nz - 1)):
        qz_copy(k).start()

    for span in range(2):
        side = y if span == 0 else 1 - y
        fresh_f[1:3] = jnp.zeros((2, 16, 128), jnp.float32)
        first = 4 * lax.rem(NY * h + y, 4)
        for w in range(NH):
            fresh_f[0] = col[side * NH + w, 16:32, :].astype(jnp.float32)
            fresh_f[1, 2 * w : 2 * w + 2, :] = fresh_f[0, pl.ds(first, 2), :]
            fresh_f[2, 2 * w : 2 * w + 2, :] = fresh_f[0, pl.ds(first + 2, 2), :]
        kf[span] = fresh_f[1].astype(jnp.bfloat16)
        vf[span] = fresh_f[2].astype(jnp.bfloat16)

    mine = ordq[z, :, pl.ds(base, 128)]
    lane = lax.broadcasted_iota(jnp.int32, (8, 128), 1)

    def key_order(side):
        hit = lax.div(lane, 16) == lax.div(tile_row, 2) + NH * side
        hit = hit & (lax.rem(lane, 2) == lax.rem(tile_row, 2))
        return jnp.max(jnp.where(hit, mine, -1.0), axis=1, keepdims=True)

    fresh_order = (key_order(y), key_order(1 - y))

    def forward(k):
        qz_arrival(k).wait_recv()
        for off in range(1, nx):
            qx_copy(k, off).start()

    def scores(span, d, s_ref, j, m):
        keys = kb[span, j * CHUNK : (j + 1) * CHUNK, :]
        s = lax.dot_general(
            keys, qall[d], (((1,), (1,)), ((), ())), preferred_element_type=jnp.float32
        )
        s = s + jnp.concatenate([bias[span, j * CHUNK : (j + 1) * CHUNK, :]] * nx, axis=1)
        s_ref[j * CHUNK : (j + 1) * CHUNK, :] = s
        top = jnp.max(s.reshape(CHUNK // 8, 8, rows), axis=0)
        return top if m is None else jnp.maximum(m, top)

    def fresh_scores(span, d, s_ref, m):
        s = lax.dot_general(
            kf[span], qall[d], (((1,), (1,)), ((), ())), preferred_element_type=jnp.float32
        )
        key = jnp.where(span == 0, fresh_order[0], fresh_order[1])
        s = jnp.where(key <= ordq[d], s[0:8, :], masked)
        s_ref[slots : slots + 8, :] = s
        return jnp.maximum(m, s)

    def weights(span, s_ref, j, peak, total):
        p = jnp.exp2(s_ref[j * CHUNK : (j + 1) * CHUNK, :] * scale2 - peak)
        total = total + jnp.sum(p.reshape(CHUNK // 8, 8, rows), axis=0)
        values = vt[span, :, j * CHUNK : (j + 1) * CHUNK]
        more = jnp.dot(values, p.astype(jnp.bfloat16), preferred_element_type=jnp.float32)
        if j == 0:
            acc[...] = more
        else:
            acc[...] += more
        return total

    def fresh_weights(span, s_ref, peak, total):
        p = jnp.exp2(s_ref[slots : slots + 8, :] * scale2 - peak)
        both = jnp.concatenate([p, jnp.zeros_like(p)], axis=0).astype(jnp.bfloat16)
        acc[...] += lax.dot_general(
            vf[span], both, (((0,), (0,)), ((), ())), preferred_element_type=jnp.float32
        )
        return total + p

    def keep_part(d, peak, total):
        total = jnp.sum(total, axis=0, keepdims=True)
        part[d, 0:width, :] = acc[...]
        part[d, width : width + 8, :] = jnp.where(wide_row == 0, peak, total)

    def whole_part(d, peak, total):
        total = jnp.sum(total, axis=0, keepdims=True)
        old = part[d, width : width + 8, :]
        new_peak = jnp.maximum(old[0:1, :], peak)
        keep = jnp.exp2(old[0:1, :] - new_peak)
        take = jnp.exp2(peak - new_peak)
        value = part[d, 0:width, :] * keep + acc[...] * take
        return value, new_peak, old[1:2, :] * keep + total * take, new_peak

    def encode(value, peak, total, peak_total):
        size = jnp.maximum(jnp.max(jnp.abs(value), axis=0, keepdims=True), 1e-30)
        power = jnp.ceil(jnp.log2(size) + peak + 1e-3) - 15.0
        power_t = jnp.ceil(jnp.log2(total) + peak_total + 1e-3) - 15.0
        units = value * jnp.exp2(peak - power)
        units = (units + 12582912.0) - 12582912.0
        whole = total * jnp.exp2(peak_total - power_t)
        high = jnp.floor(whole)
        low = jnp.floor((whole - high) * 32767.0)
        row = lax.broadcasted_iota(jnp.int32, (16, value.shape[1]), 0)
        tail = jnp.where(row == 0, power, jnp.where(row == 1, power_t, high))
        tail = jnp.where(row == 3, low, tail)
        both = [item.astype(jnp.int32).astype(jnp.int16) for item in (units, tail)]
        return both

    def decode(ref):
        tail = ref[width : width + 16, :].astype(jnp.int32).astype(jnp.float32)
        total = tail[2:3, :] + tail[3:4, :] * (1.0 / 32767.0)
        value = ref[0:width, :].astype(jnp.int32).astype(jnp.float32)
        return value, tail[0:1, :], total, tail[1:2, :]

    def merged(items):
        peak = functools.reduce(jnp.maximum, [item[1] for item in items])
        peak_total = functools.reduce(jnp.maximum, [item[3] for item in items])
        value = sum(item[0] * jnp.exp2(item[1] - peak) for item in items)
        total = sum(item[2] * jnp.exp2(item[3] - peak_total) for item in items)
        return value, peak, total, peak_total

    def put_part(k, item):
        units, tail = encode(*item)
        for w in range(nx):
            side = slice(w * 128, (w + 1) * 128)
            xout[k, w, 0:width, :] = units[:, side]
            xout[k, w, width : width + 16, :] = tail[:, side]

    def put_own_part(item):
        for w in range(nx):
            side = slice(w * 128, (w + 1) * 128)
            items = [tuple(array[:, side] for array in item)]
            items += [decode(zfull.at[k, w]) for k in range(2)]
            units, tail = encode(*merged(items))
            xout[nz - 1, w, 0:width, :] = units
            xout[nz - 1, w, width : width + 16, :] = tail

    def order_of(t):
        first = jnp.where(t <= nz - 3, nz - 1 - t, t - (nz - 2))
        return jnp.where(t < nz, first, t - nz)

    def step(t, span, s_now, s_next, m, ahead=True, own_plane=False):
        k = order_of(t)
        d = plane(k)
        span_n, d_n = lax.div(t + 1, nz), plane(order_of(t + 1))
        peak = jnp.max(m, axis=0, keepdims=True) * scale2
        total = jnp.zeros((8, rows), jnp.float32)
        nxt = None
        for j in range(chunks):
            if ahead:
                nxt = scores(span_n, d_n, s_next, j, nxt)
            total = weights(span, s_now, j, peak, total)
        if ahead:
            nxt = fresh_scores(span_n, d_n, s_next, nxt)
        total = fresh_weights(span, s_now, peak, total)
        if span == 0:
            keep_part(d, peak, total)
        elif own_plane:
            for j in range(2):
                pf_arrival(j).wait_recv()
            put_own_part(whole_part(d, peak, total))
        else:
            put_part(k, whole_part(d, peak, total))
        return nxt

    def px_copy(k, off):
        who = lax.rem(x + off, nx)
        return remote(xout.at[k, who], xin.at[k, off], px_s.at[k, off], px_r.at[k, off], at(h, who, y, z))

    def px_arrival(k, off):
        who = lax.rem(x + nx - off, nx)
        return remote(xout.at[k, who], xin.at[k, off], px_s.at[k, off], px_r.at[k, off], at(h, who, y, z))

    def pf_copy(k):
        return remote(xout.at[k], zfull.at[k], pz_s.at[k], pz_r.at[k], at(h, x, y, plane(k)))

    def pf_arrival(k):
        who = lax.rem(z + nz - far(k), nz)
        return remote(xout.at[k], zfull.at[k], pz_s.at[k], pz_r.at[k], at(h, x, y, who))

    def pz_copy(k):
        return remote(zout.at[k], zin.at[k], pz_s.at[k], pz_r.at[k], at(h, x, y, plane(k)))

    def pz_arrival(k):
        who = lax.rem(z + nz - far(k), nz)
        return remote(zout.at[k], zin.at[k], pz_s.at[k], pz_r.at[k], at(h, x, y, who))

    def send_x(k):
        for off in range(1, nx):
            px_copy(k, off).start()

    def merge_x(k):
        items = [decode(xout.at[k, x])]
        for off in range(1, nx):
            px_arrival(k, off).wait_recv()
        items += [decode(xin.at[k, off]) for off in range(1, nx)]
        return merged(items)

    def send_z(k):
        units, tail = encode(*merge_x(k))
        zout[k, 0:width, :] = units
        zout[k, width : width + 16, :] = tail
        pz_copy(k).start()

    def need_x(k):
        for off in range(1, nx):
            qx_arrival(k, off).wait_recv()

    def before(t):
        @pl.when(t + 4 <= nz - 3)
        def _():
            forward(nz - 5 - t)

        @pl.when(t + 1 <= nz - 3)
        def _():
            need_x(nz - 2 - t)

        @pl.when((t + 1 > nz - 3) & (t + 1 < nz))
        def _():
            qf_arrival(t + 1 - (nz - 2)).wait_recv()

        @pl.when(t + 1 == nz)
        def _():
            len_copy.wait_recv()
            kv[0].wait_recv()
            set_bias(1, plen[0:1, :])

    def after(k):
        @pl.when(k < 2)
        def _():
            pf_copy(k).start()

        @pl.when(k >= 2)
        def _():
            send_x(k)

        @pl.when(k >= 2 + LAG)
        def _():
            send_z(k - LAG)

    need_x(nz - 1)
    for k in range(2):
        qf_copy(k).start()
    m = None
    for j in range(chunks):
        m = scores(0, z, s_a, j, m)
    m = fresh_scores(0, z, s_a, m)
    for t in range(1, min(4, nz - 2)):
        forward(nz - 1 - t)

    def pair0(i, m):
        t = 2 * i
        before(t)
        m = step(t, 0, s_a, s_b, m)
        before(t + 1)
        return step(t + 1, 0, s_b, s_a, m)

    m = lax.fori_loop(0, nz // 2, pair0, m)

    ahead = None
    for j in range(chunks):
        ahead = scores(1, plane(1), s_b, j, ahead)
    ahead = fresh_scores(1, plane(1), s_b, ahead)
    kv[1].wait_recv()
    step(nz, 1, s_a, s_b, m, ahead=False)
    after(0)
    m = step(nz + 1, 1, s_b, s_a, ahead)
    after(1)

    def pair1(i, m):
        k = 2 * i
        m = step(nz + k, 1, s_a, s_b, m)
        after(k)
        m = step(nz + k + 1, 1, s_b, s_a, m)
        after(k + 1)
        return m

    m = lax.fori_loop(1, nz // 2 - 1, pair1, m)
    m = step(2 * nz - 2, 1, s_a, s_b, m)
    after(nz - 2)
    step(2 * nz - 1, 1, s_b, s_a, m, ahead=False, own_plane=True)
    after(nz - 1)
    for k in range(max(nz - LAG, 2), nz - 1):
        send_z(k)

    items = [merge_x(nz - 1)]
    for k in range(2, nz - 1):
        pz_arrival(k).wait_recv()
        items.append(decode(zin.at[k]))
    value, peak, total, peak_total = merged(items)
    value = value * (jnp.exp2(peak - peak_total) / total)
    fout[...] = value.T.astype(jnp.bfloat16)

    def home(off):
        w, h_, y_ = col_peer(off)
        src = fout.at[pl.ds(pl.multiple_of(w * 16, 16), 16), :]
        return remote(src, out.at[NY * h + y], f_s.at[w], f_r.at[u], at(h_, x, y_, z))

    def home_arrival(off):
        w, h_, y_ = col_peer(off)
        src = fout.at[pl.ds(0, 16), :]
        return remote(src, out.at[NY * h_ + y_], f_s.at[w], f_r.at[w], at(h_, x, y_, z))

    for off in FAR_FIRST:
        home(off).start()
    rest = pltpu.make_async_copy(
        fout.at[pl.ds(pl.multiple_of(u * 16, 16), 16), :], out.at[NY * h + y], own_sem.at[0]
    )
    rest.start()

    for off in range(1, COL):
        col_copy(off).wait_send()
    len_copy.wait_send()
    for copy in kv:
        copy.wait_send()
    for k in range(nz):
        if k >= 2:
            for off in range(1, nx):
                qx_copy(k, off).wait_send()
                px_copy(k, off).wait_send()
        if k < 2:
            qf_copy(k).wait_send()
            pf_copy(k).wait_send()
        elif k < nz - 1:
            qz_copy(k).wait_send()
            pz_copy(k).wait_send()
    for off in range(1, COL):
        home_arrival(off).wait_recv()
    rest.wait()
    for off in range(1, COL):
        home(off).wait_send()


def shards(nx, nz, q_new, kv_new, k_cache, v_cache, span_len, order):
    kv_dev, slots, width = k_cache.shape
    tokens = q_new.shape[0]
    kv_heads = NH * kv_dev
    group = q_new.shape[1] // (kv_heads * width)
    rows = 128 * nx
    bf = jnp.bfloat16
    queries = q_new.reshape(tokens, kv_heads * group, width).transpose(1, 0, 2)
    queries = queries.reshape(kv_heads * group * tokens, width)
    fresh = kv_new.reshape(tokens, kv_heads * 2, width).transpose(1, 0, 2)
    fresh = fresh.reshape(kv_heads * 2 * tokens, width)
    places = order.reshape(NH, -1)
    scale2 = width ** (-0.5) * 1.4426950408889634
    hbm = pl.BlockSpec(memory_space=pltpu.HBM)
    i16 = jnp.int16
    f32 = jnp.float32
    dma = pltpu.SemaphoreType.DMA
    out = pl.pallas_call(
        functools.partial(kernel, nx, nz, scale2),
        out_shape=jax.ShapeDtypeStruct((kv_heads, tokens * group, width), bf),
        in_specs=[hbm] * 6,
        out_specs=hbm,
        scratch_shapes=[
            pltpu.VMEM(queries.shape, bf),
            pltpu.VMEM(fresh.shape, bf),
            pltpu.VMEM(places.shape, jnp.int32),
            pltpu.SMEM(span_len.shape, jnp.int32),
            pltpu.VMEM((COL, 32, width), bf),
            pltpu.VMEM((nz, 8, rows), f32),
            pltpu.VMEM((8, 128), f32),
            pltpu.VMEM((COL, 32, width), bf),
            pltpu.VMEM((nz, rows, width), bf),
            pltpu.VMEM((2, slots, width), bf),
            pltpu.VMEM((2, slots, width), bf),
            pltpu.VMEM((2, width, slots), bf),
            pltpu.VMEM((width, slots), bf),
            pltpu.VMEM((2, 16, width), bf),
            pltpu.VMEM((2, 16, width), bf),
            pltpu.VMEM((3, 16, width), f32),
            pltpu.VMEM((2, slots, 128), f32),
            pltpu.VMEM((8, 128), f32),
            pltpu.VMEM((slots + 8, rows), f32),
            pltpu.VMEM((slots + 8, rows), f32),
            pltpu.VMEM((width, rows), f32),
            pltpu.VMEM((nz, width + 8, rows), f32),
            pltpu.VMEM((nz, nx, width + 16, 128), i16),
            pltpu.VMEM((nz, nx, width + 16, 128), i16),
            pltpu.VMEM((2, nx, width + 16, 128), i16),
            pltpu.VMEM((nz, width + 16, 128), i16),
            pltpu.VMEM((nz, width + 16, 128), i16),
            pltpu.VMEM((128, width), bf),
            dma((COL,)), dma((COL,)), dma, dma, dma((2,)), dma((2,)), dma((6,)),
            dma((nz,)), dma((nz,)), dma((nz, nx)), dma((nz, nx)),
            dma((nz, nx)), dma((nz, nx)), dma((nz,)), dma((nz,)), dma((COL,)), dma((COL,)),
        ],
        compiler_params=pltpu.CompilerParams(
            collective_id=0, has_side_effects=True, vmem_limit_bytes=62 << 20
        ),
    )(queries, fresh, span_len, places, k_cache, v_cache)
    out = out.reshape(kv_heads * group, tokens, width).transpose(1, 0, 2)
    return out.reshape(tokens, kv_heads * group * width)


def solution(mesh):
    nz = 8
    nx = mesh.shape["ctx"] // (nz * NY)
    return jax.shard_map(
        functools.partial(shards, nx, nz),
        mesh=mesh,
        in_specs=(
            P(("head", "ctx"), None),
            P(("head", "ctx"), None),
            P("head", "ctx", None),
            P("head", "ctx", None),
            P("ctx"),
            P(),
        ),
        out_specs=P(("head", "ctx"), None),
        check_vma=False,
    )
```

```python
import functools

import jax
import jax.numpy as jnp
from jax import lax
from jax.experimental import pallas as pl
from jax.experimental.pallas import tpu as pltpu
from jax.sharding import PartitionSpec as P

MESH = pl.DeviceIdType.MESH
masked = -1e30
NH = 4
NY = 2
COL = NH * NY
FAR_FIRST = (2, 6, 3, 5, 1, 7, 4)
CHUNK = 256
LAG = 3


def kernel(
    nx, nz, scale2,
    q_hbm, f_hbm, len_hbm, ord_hbm, k_hbm, v_hbm,
    out,
    q_in, f_in, ord_in, len_smem, msg, ordq, lens,
    col, qall, kb, vb, vt, vo, kf, vf, fresh_f, bias, plen, s_a, s_b, acc, part,
    xout, xin, zfull, zout, zin, fout,
    col_s, col_r, len_s, len_r, kv_s, kv_r, own_sem, qz_s, qz_r, qx_s, qx_r,
    px_s, px_r, pz_s, pz_r, f_s, f_r,
):
    h = lax.axis_index("head")
    c = lax.axis_index("ctx")
    z = lax.rem(c, nz)
    y = lax.rem(lax.div(c, nz), NY)
    x = lax.div(c, nz * NY)
    u = y * NH + h
    slots = k_hbm.shape[1]
    rows = 128 * nx
    width = k_hbm.shape[2]
    chunks = slots // CHUNK

    def at(h_, x_, y_, z_):
        return (h_, (x_ * NY + y_) * nz + z_)

    def col_peer(off):
        w = lax.rem(u + off, COL)
        return w, lax.rem(w, NH), lax.div(w, NH)

    def remote(src, dst, ss, rs, dev):
        return pltpu.make_async_remote_copy(
            src_ref=src, dst_ref=dst, send_sem=ss, recv_sem=rs, device_id=dev, device_id_type=MESH
        )

    def far(k):
        half = lax.div(k - 2, 2)
        rest = jnp.where(lax.rem(k, 2) == 0, nz // 2 + half, nz // 2 - 1 - half)
        return jnp.where(k == 0, 1, jnp.where(k == 1, nz - 1, jnp.where(k == nz - 1, 0, rest)))

    def plane(t):
        return lax.rem(z + far(t), nz)

    own = [
        pltpu.make_async_copy(k_hbm.at[y], kb.at[0], own_sem.at[0]),
        pltpu.make_async_copy(v_hbm, vb, own_sem.at[1]),
    ]
    small = [
        pltpu.make_async_copy(q_hbm, q_in, own_sem.at[2]),
        pltpu.make_async_copy(f_hbm, f_in, own_sem.at[3]),
        pltpu.make_async_copy(ord_hbm, ord_in, own_sem.at[4]),
        pltpu.make_async_copy(len_hbm, len_smem, own_sem.at[5]),
    ]
    for copy in small + own:
        copy.start()

    barrier = pltpu.get_barrier_semaphore()
    for off in range(1, COL):
        _, h_, y_ = col_peer(off)
        pl.semaphore_signal(barrier, inc=1, device_id=at(h_, x, y_, z), device_id_type=MESH)
    for off in range(1, nz):
        pl.semaphore_signal(
            barrier, inc=1, device_id=at(h, x, y, lax.rem(z + off, nz)), device_id_type=MESH
        )
    for off in range(1, nx):
        pl.semaphore_signal(
            barrier, inc=1, device_id=at(h, lax.rem(x + off, nx), y, z), device_id_type=MESH
        )

    tile_row = lax.broadcasted_iota(jnp.int32, (8, 128), 0)
    wide_row = lax.broadcasted_iota(jnp.int32, (8, rows), 0)
    for copy in small:
        copy.wait()
    lens[...] = jnp.zeros((8, 128), jnp.float32) + len_smem[0].astype(jnp.float32)

    def set_bias(span, length):
        for j in range(chunks):
            slot = lax.broadcasted_iota(jnp.int32, (CHUNK, 128), 0).astype(jnp.float32) + j * CHUNK
            bias[span, j * CHUNK : (j + 1) * CHUNK, :] = jnp.where(slot < length, 0.0, masked)

    set_bias(0, lens[0:1, :])
    for w in range(COL):
        msg[w, 0:16, :] = q_in[w * 16 : (w + 1) * 16, :]
        msg[w, 16:32, :] = f_in[w // 4 * 16 : w // 4 * 16 + 16, :]

    places = ord_in.shape[1]
    pos = ord_in[...]
    high, low = lax.div(pos, 16), lax.rem(pos, 16)
    digits = jnp.concatenate([high, low], axis=0).astype(jnp.float32).astype(jnp.bfloat16)
    lane = lax.broadcasted_iota(jnp.int32, (places, rows), 1)
    place = lax.broadcasted_iota(jnp.int32, (places, rows), 0)
    source = lax.div(lane, 64) * (2 * nz) + lax.rem(lane, 2)
    lane8 = lax.broadcasted_iota(jnp.int32, (8, rows), 1)
    picked = lax.rem(lax.div(lane8, 16), NH) == lax.rem(lax.broadcasted_iota(jnp.int32, (8, rows), 0), NH)
    for d in range(nz):
        pick = jnp.where(place == source + 2 * d, 1.0, 0.0).astype(jnp.bfloat16)
        both = jnp.dot(digits, pick, preferred_element_type=jnp.float32)
        both = jnp.where(picked, both, 0.0) * jnp.where(
            lax.broadcasted_iota(jnp.int32, (8, rows), 0) < NH, 16.0, 1.0
        )
        ordq[d] = jnp.broadcast_to(jnp.sum(both, axis=0, keepdims=True), (8, rows))

    for copy in own:
        copy.wait()
    for j in range(slots // 128):
        cut = slice(j * 128, (j + 1) * 128)
        vt[0, :, cut] = vb[y, cut, :].T
        vo[:, cut] = vb[1 - y, cut, :].T

    pl.semaphore_wait(barrier, COL + nz + nx - 3)

    def col_copy(off):
        w, h_, y_ = col_peer(off)
        return remote(
            msg.at[NY * h_ + y_], col.at[u], col_s.at[w], col_r.at[u], at(h_, x, y_, z)
        )

    def col_arrival(off):
        w, h_, y_ = col_peer(off)
        return remote(msg.at[0], col.at[w], col_s.at[w], col_r.at[w], at(h_, x, y_, z))

    for off in FAR_FIRST:
        col_copy(off).start()
    partner = at(h, x, 1 - y, z)
    len_copy = remote(lens, plen, len_s, len_r, partner)
    len_copy.start()
    kv = [
        remote(k_hbm.at[1 - y], kb.at[1], kv_s.at[0], kv_r.at[0], partner),
        remote(vo, vt.at[1], kv_s.at[1], kv_r.at[1], partner),
    ]
    for copy in kv:
        copy.start()
    col[u] = msg[NY * h + y]

    for off in range(1, COL):
        col_arrival(off).wait_recv()

    base = pl.multiple_of(x * 128, 128)
    for w in range(COL):
        qall[z, pl.ds(pl.multiple_of(x * 128 + w * 16, 16), 16), :] = col[w, 0:16, :]

    def qz_copy(t):
        to = lax.rem(z + nz - far(t), nz)
        ref = qall.at[z, pl.ds(base, 128), :]
        return remote(ref, ref, qz_s.at[t], qz_r.at[t], at(h, x, y, to))

    def qf_copy(k):
        to = lax.rem(z + nz - far(k), nz)
        return remote(qall.at[z], qall.at[z], qz_s.at[k], qz_r.at[k], at(h, x, y, to))

    def qf_arrival(k):
        ref = qall.at[plane(k)]
        return remote(ref, ref, qz_s.at[k], qz_r.at[k], at(h, x, y, plane(k)))

    def qz_arrival(t):
        ref = qall.at[plane(t), pl.ds(base, 128), :]
        return remote(ref, ref, qz_s.at[t], qz_r.at[t], at(h, x, y, plane(t)))

    def qx_copy(t, off):
        ref = qall.at[plane(t), pl.ds(base, 128), :]
        return remote(
            ref, ref, qx_s.at[t, off], qx_r.at[t, off], at(h, lax.rem(x + off, nx), y, z)
        )

    def qx_arrival(t, off):
        who = lax.rem(x + nx - off, nx)
        ref = qall.at[plane(t), pl.ds(pl.multiple_of(who * 128, 128), 128), :]
        return remote(ref, ref, qx_s.at[t, off], qx_r.at[t, off], at(h, who, y, z))

    for off in range(1, nx):
        qx_copy(nz - 1, off).start()
    for k in reversed(range(2, nz - 1)):
        qz_copy(k).start()

    for span in range(2):
        side = y if span == 0 else 1 - y
        fresh_f[1:3] = jnp.zeros((2, 16, 128), jnp.float32)
        first = 4 * lax.rem(NY * h + y, 4)
        for w in range(NH):
            fresh_f[0] = col[side * NH + w, 16:32, :].astype(jnp.float32)
            fresh_f[1, 2 * w : 2 * w + 2, :] = fresh_f[0, pl.ds(first, 2), :]
            fresh_f[2, 2 * w : 2 * w + 2, :] = fresh_f[0, pl.ds(first + 2, 2), :]
        kf[span] = fresh_f[1].astype(jnp.bfloat16)
        vf[span] = fresh_f[2].astype(jnp.bfloat16)

    mine = ordq[z, :, pl.ds(base, 128)]
    lane = lax.broadcasted_iota(jnp.int32, (8, 128), 1)

    def key_order(side):
        hit = lax.div(lane, 16) == lax.div(tile_row, 2) + NH * side
        hit = hit & (lax.rem(lane, 2) == lax.rem(tile_row, 2))
        return jnp.max(jnp.where(hit, mine, -1.0), axis=1, keepdims=True)

    fresh_order = (key_order(y), key_order(1 - y))

    def forward(k):
        qz_arrival(k).wait_recv()
        for off in range(1, nx):
            qx_copy(k, off).start()

    def scores(span, d, s_ref, j, m):
        keys = kb[span, j * CHUNK : (j + 1) * CHUNK, :]
        s = lax.dot_general(
            keys, qall[d], (((1,), (1,)), ((), ())), preferred_element_type=jnp.float32
        )
        s = s + jnp.concatenate([bias[span, j * CHUNK : (j + 1) * CHUNK, :]] * nx, axis=1)
        s_ref[j * CHUNK : (j + 1) * CHUNK, :] = s
        top = jnp.max(s.reshape(CHUNK // 8, 8, rows), axis=0)
        return top if m is None else jnp.maximum(m, top)

    def fresh_scores(span, d, s_ref, m):
        s = lax.dot_general(
            kf[span], qall[d], (((1,), (1,)), ((), ())), preferred_element_type=jnp.float32
        )
        key = jnp.where(span == 0, fresh_order[0], fresh_order[1])
        s = jnp.where(key <= ordq[d], s[0:8, :], masked)
        s_ref[slots : slots + 8, :] = s
        return jnp.maximum(m, s)

    def weights(span, s_ref, j, peak, total):
        p = jnp.exp2(s_ref[j * CHUNK : (j + 1) * CHUNK, :] * scale2 - peak)
        total = total + jnp.sum(p.reshape(CHUNK // 8, 8, rows), axis=0)
        values = vt[span, :, j * CHUNK : (j + 1) * CHUNK]
        more = jnp.dot(values, p.astype(jnp.bfloat16), preferred_element_type=jnp.float32)
        if j == 0:
            acc[...] = more
        else:
            acc[...] += more
        return total

    def fresh_weights(span, s_ref, peak, total):
        p = jnp.exp2(s_ref[slots : slots + 8, :] * scale2 - peak)
        both = jnp.concatenate([p, jnp.zeros_like(p)], axis=0).astype(jnp.bfloat16)
        acc[...] += lax.dot_general(
            vf[span], both, (((0,), (0,)), ((), ())), preferred_element_type=jnp.float32
        )
        return total + p

    def keep_part(d, peak, total):
        total = jnp.sum(total, axis=0, keepdims=True)
        part[d, 0:width, :] = acc[...]
        part[d, width : width + 8, :] = jnp.where(wide_row == 0, peak, total)

    def whole_part(d, peak, total):
        total = jnp.sum(total, axis=0, keepdims=True)
        old = part[d, width : width + 8, :]
        new_peak = jnp.maximum(old[0:1, :], peak)
        keep = jnp.exp2(old[0:1, :] - new_peak)
        take = jnp.exp2(peak - new_peak)
        value = part[d, 0:width, :] * keep + acc[...] * take
        return value, new_peak, old[1:2, :] * keep + total * take, new_peak

    def encode(value, peak, total, peak_total):
        size = jnp.maximum(jnp.max(jnp.abs(value), axis=0, keepdims=True), 1e-30)
        power = jnp.ceil(jnp.log2(size) + peak + 1e-3) - 15.0
        power_t = jnp.ceil(jnp.log2(total) + peak_total + 1e-3) - 15.0
        units = value * jnp.exp2(peak - power)
        units = (units + 12582912.0) - 12582912.0
        whole = total * jnp.exp2(peak_total - power_t)
        high = jnp.floor(whole)
        low = jnp.floor((whole - high) * 32767.0)
        row = lax.broadcasted_iota(jnp.int32, (16, value.shape[1]), 0)
        tail = jnp.where(row == 0, power, jnp.where(row == 1, power_t, high))
        tail = jnp.where(row == 3, low, tail)
        both = [item.astype(jnp.int32).astype(jnp.int16) for item in (units, tail)]
        return both

    def decode(ref):
        tail = ref[width : width + 16, :].astype(jnp.int32).astype(jnp.float32)
        total = tail[2:3, :] + tail[3:4, :] * (1.0 / 32767.0)
        value = ref[0:width, :].astype(jnp.int32).astype(jnp.float32)
        return value, tail[0:1, :], total, tail[1:2, :]

    def merged(items):
        peak = functools.reduce(jnp.maximum, [item[1] for item in items])
        peak_total = functools.reduce(jnp.maximum, [item[3] for item in items])
        value = sum(item[0] * jnp.exp2(item[1] - peak) for item in items)
        total = sum(item[2] * jnp.exp2(item[3] - peak_total) for item in items)
        return value, peak, total, peak_total

    def put_part(k, item):
        units, tail = encode(*item)
        for w in range(nx):
            side = slice(w * 128, (w + 1) * 128)
            xout[k, w, 0:width, :] = units[:, side]
            xout[k, w, width : width + 16, :] = tail[:, side]

    def put_own_part(item):
        for w in range(nx):
            side = slice(w * 128, (w + 1) * 128)
            items = [tuple(array[:, side] for array in item)]
            items += [decode(zfull.at[k, w]) for k in range(2)]
            units, tail = encode(*merged(items))
            xout[nz - 1, w, 0:width, :] = units
            xout[nz - 1, w, width : width + 16, :] = tail

    def order_of(t):
        first = jnp.where(t <= nz - 3, nz - 1 - t, t - (nz - 2))
        return jnp.where(t < nz, first, t - nz)

    def step(t, span, s_now, s_next, m, ahead=True, own_plane=False):
        k = order_of(t)
        d = plane(k)
        span_n, d_n = lax.div(t + 1, nz), plane(order_of(t + 1))
        peak = jnp.max(m, axis=0, keepdims=True) * scale2
        total = jnp.zeros((8, rows), jnp.float32)
        nxt = None
        for j in range(chunks):
            if ahead:
                nxt = scores(span_n, d_n, s_next, j, nxt)
            total = weights(span, s_now, j, peak, total)
        if ahead:
            nxt = fresh_scores(span_n, d_n, s_next, nxt)
        total = fresh_weights(span, s_now, peak, total)
        if span == 0:
            keep_part(d, peak, total)
        elif own_plane:
            for j in range(2):
                pf_arrival(j).wait_recv()
            put_own_part(whole_part(d, peak, total))
        else:
            put_part(k, whole_part(d, peak, total))
        return nxt

    def px_copy(k, off):
        who = lax.rem(x + off, nx)
        return remote(xout.at[k, who], xin.at[k, off], px_s.at[k, off], px_r.at[k, off], at(h, who, y, z))

    def px_arrival(k, off):
        who = lax.rem(x + nx - off, nx)
        return remote(xout.at[k, who], xin.at[k, off], px_s.at[k, off], px_r.at[k, off], at(h, who, y, z))

    def pf_copy(k):
        return remote(xout.at[k], zfull.at[k], pz_s.at[k], pz_r.at[k], at(h, x, y, plane(k)))

    def pf_arrival(k):
        who = lax.rem(z + nz - far(k), nz)
        return remote(xout.at[k], zfull.at[k], pz_s.at[k], pz_r.at[k], at(h, x, y, who))

    def pz_copy(k):
        return remote(zout.at[k], zin.at[k], pz_s.at[k], pz_r.at[k], at(h, x, y, plane(k)))

    def pz_arrival(k):
        who = lax.rem(z + nz - far(k), nz)
        return remote(zout.at[k], zin.at[k], pz_s.at[k], pz_r.at[k], at(h, x, y, who))

    def send_x(k):
        for off in range(1, nx):
            px_copy(k, off).start()

    def merge_x(k):
        items = [decode(xout.at[k, x])]
        for off in range(1, nx):
            px_arrival(k, off).wait_recv()
        items += [decode(xin.at[k, off]) for off in range(1, nx)]
        return merged(items)

    def send_z(k):
        units, tail = encode(*merge_x(k))
        zout[k, 0:width, :] = units
        zout[k, width : width + 16, :] = tail
        pz_copy(k).start()

    def need_x(k):
        for off in range(1, nx):
            qx_arrival(k, off).wait_recv()

    def before(t):
        @pl.when(t + 4 <= nz - 3)
        def _():
            forward(nz - 5 - t)

        @pl.when(t + 1 <= nz - 3)
        def _():
            need_x(nz - 2 - t)

        @pl.when((t + 1 > nz - 3) & (t + 1 < nz))
        def _():
            qf_arrival(t + 1 - (nz - 2)).wait_recv()

        @pl.when(t + 1 == nz)
        def _():
            len_copy.wait_recv()
            kv[0].wait_recv()
            set_bias(1, plen[0:1, :])

    def after(k):
        @pl.when(k < 2)
        def _():
            pf_copy(k).start()

        @pl.when(k >= 2)
        def _():
            send_x(k)

        @pl.when(k >= 2 + LAG)
        def _():
            send_z(k - LAG)

    need_x(nz - 1)
    for k in range(2):
        qf_copy(k).start()
    m = None
    for j in range(chunks):
        m = scores(0, z, s_a, j, m)
    m = fresh_scores(0, z, s_a, m)
    for t in range(1, min(4, nz - 2)):
        forward(nz - 1 - t)

    def pair0(i, m):
        t = 2 * i
        before(t)
        m = step(t, 0, s_a, s_b, m)
        before(t + 1)
        return step(t + 1, 0, s_b, s_a, m)

    m = lax.fori_loop(0, nz // 2, pair0, m)

    ahead = None
    for j in range(chunks):
        ahead = scores(1, plane(1), s_b, j, ahead)
    ahead = fresh_scores(1, plane(1), s_b, ahead)
    kv[1].wait_recv()
    step(nz, 1, s_a, s_b, m, ahead=False)
    after(0)
    m = step(nz + 1, 1, s_b, s_a, ahead)
    after(1)

    def pair1(i, m):
        k = 2 * i
        m = step(nz + k, 1, s_a, s_b, m)
        after(k)
        m = step(nz + k + 1, 1, s_b, s_a, m)
        after(k + 1)
        return m

    m = lax.fori_loop(1, nz // 2 - 1, pair1, m)
    m = step(2 * nz - 2, 1, s_a, s_b, m)
    after(nz - 2)
    step(2 * nz - 1, 1, s_b, s_a, m, ahead=False, own_plane=True)
    after(nz - 1)
    for k in range(max(nz - LAG, 2), nz - 1):
        send_z(k)

    items = [merge_x(nz - 1)]
    for k in range(2, nz - 2):
        pz_arrival(k).wait_recv()
        items.append(decode(zin.at[k]))
    items = [merged(items)]
    pz_arrival(nz - 2).wait_recv()
    items.append(decode(zin.at[nz - 2]))
    value, peak, total, peak_total = merged(items)
    value = value * (jnp.exp2(peak - peak_total) / total)
    fout[...] = value.T.astype(jnp.bfloat16)

    def home(off):
        w, h_, y_ = col_peer(off)
        src = fout.at[pl.ds(pl.multiple_of(w * 16, 16), 16), :]
        return remote(src, out.at[NY * h + y], f_s.at[w], f_r.at[u], at(h_, x, y_, z))

    def home_arrival(off):
        w, h_, y_ = col_peer(off)
        src = fout.at[pl.ds(0, 16), :]
        return remote(src, out.at[NY * h_ + y_], f_s.at[w], f_r.at[w], at(h_, x, y_, z))

    for off in FAR_FIRST:
        home(off).start()
    rest = pltpu.make_async_copy(
        fout.at[pl.ds(pl.multiple_of(u * 16, 16), 16), :], out.at[NY * h + y], own_sem.at[0]
    )
    rest.start()

    for off in range(1, COL):
        col_copy(off).wait_send()
    len_copy.wait_send()
    for copy in kv:
        copy.wait_send()
    for k in range(nz):
        if k >= 2:
            for off in range(1, nx):
                qx_copy(k, off).wait_send()
                px_copy(k, off).wait_send()
        if k < 2:
            qf_copy(k).wait_send()
            pf_copy(k).wait_send()
        elif k < nz - 1:
            qz_copy(k).wait_send()
            pz_copy(k).wait_send()
    for off in range(1, COL):
        home_arrival(off).wait_recv()
    rest.wait()
    for off in range(1, COL):
        home(off).wait_send()


def shards(nx, nz, q_new, kv_new, k_cache, v_cache, span_len, order):
    kv_dev, slots, width = k_cache.shape
    tokens = q_new.shape[0]
    kv_heads = NH * kv_dev
    group = q_new.shape[1] // (kv_heads * width)
    rows = 128 * nx
    bf = jnp.bfloat16
    queries = q_new.reshape(tokens, kv_heads * group, width).transpose(1, 0, 2)
    queries = queries.reshape(kv_heads * group * tokens, width)
    fresh = kv_new.reshape(tokens, kv_heads * 2, width).transpose(1, 0, 2)
    fresh = fresh.reshape(kv_heads * 2 * tokens, width)
    places = order.reshape(NH, -1)
    scale2 = width ** (-0.5) * 1.4426950408889634
    hbm = pl.BlockSpec(memory_space=pltpu.HBM)
    i16 = jnp.int16
    f32 = jnp.float32
    dma = pltpu.SemaphoreType.DMA
    out = pl.pallas_call(
        functools.partial(kernel, nx, nz, scale2),
        out_shape=jax.ShapeDtypeStruct((kv_heads, tokens * group, width), bf),
        in_specs=[hbm] * 6,
        out_specs=hbm,
        scratch_shapes=[
            pltpu.VMEM(queries.shape, bf),
            pltpu.VMEM(fresh.shape, bf),
            pltpu.VMEM(places.shape, jnp.int32),
            pltpu.SMEM(span_len.shape, jnp.int32),
            pltpu.VMEM((COL, 32, width), bf),
            pltpu.VMEM((nz, 8, rows), f32),
            pltpu.VMEM((8, 128), f32),
            pltpu.VMEM((COL, 32, width), bf),
            pltpu.VMEM((nz, rows, width), bf),
            pltpu.VMEM((2, slots, width), bf),
            pltpu.VMEM((2, slots, width), bf),
            pltpu.VMEM((2, width, slots), bf),
            pltpu.VMEM((width, slots), bf),
            pltpu.VMEM((2, 16, width), bf),
            pltpu.VMEM((2, 16, width), bf),
            pltpu.VMEM((3, 16, width), f32),
            pltpu.VMEM((2, slots, 128), f32),
            pltpu.VMEM((8, 128), f32),
            pltpu.VMEM((slots + 8, rows), f32),
            pltpu.VMEM((slots + 8, rows), f32),
            pltpu.VMEM((width, rows), f32),
            pltpu.VMEM((nz, width + 8, rows), f32),
            pltpu.VMEM((nz, nx, width + 16, 128), i16),
            pltpu.VMEM((nz, nx, width + 16, 128), i16),
            pltpu.VMEM((2, nx, width + 16, 128), i16),
            pltpu.VMEM((nz, width + 16, 128), i16),
            pltpu.VMEM((nz, width + 16, 128), i16),
            pltpu.VMEM((128, width), bf),
            dma((COL,)), dma((COL,)), dma, dma, dma((2,)), dma((2,)), dma((6,)),
            dma((nz,)), dma((nz,)), dma((nz, nx)), dma((nz, nx)),
            dma((nz, nx)), dma((nz, nx)), dma((nz,)), dma((nz,)), dma((COL,)), dma((COL,)),
        ],
        compiler_params=pltpu.CompilerParams(
            collective_id=0, has_side_effects=True, vmem_limit_bytes=62 << 20
        ),
    )(queries, fresh, span_len, places, k_cache, v_cache)
    out = out.reshape(kv_heads * group, tokens, width).transpose(1, 0, 2)
    return out.reshape(tokens, kv_heads * group * width)


def solution(mesh):
    nz = 8
    nx = mesh.shape["ctx"] // (nz * NY)
    return jax.shard_map(
        functools.partial(shards, nx, nz),
        mesh=mesh,
        in_specs=(
            P(("head", "ctx"), None),
            P(("head", "ctx"), None),
            P("head", "ctx", None),
            P("head", "ctx", None),
            P("ctx"),
            P(),
        ),
        out_specs=P(("head", "ctx"), None),
        check_vma=False,
    )
```
